512 devices in a mesh: ctx: 64 (over x, z, core), vocab: 8 (over y).
Axes of the slice: x: 4, y: 8, z: 8, core: 2. Of those that a mesh axis runs over, the one named last changes fastest.
Arguments:
- hidden: bfloat16 [16384, 8192], P('ctx', 'vocab'), may hold values from -540 to 540
- norm_gain: float32 [8192], P('vocab'), may hold values from 0.5 to 1.5
- head: bfloat16 [63232, 8192], P('ctx', 'vocab'), may hold values from -0.53033009 to 0.53033009
- masked_pos: int32 [2, 64], replicated, may hold values from 0 to 8191, as said below
- masked_targets: int32 [2, 64], replicated, may hold values from 0 to 63231
- t_num: int32 [2], replicated, may hold values from 1 to 3, as said below
- t_den: int32 [2], replicated, may hold values from 192 to 319
Outputs:
- loss_value: float32 [], replicated
- grad_hidden: bfloat16 [16384, 8192], P('ctx', 'vocab')
- grad_head: bfloat16 [63232, 8192], P('ctx', 'vocab')
- grad_gain: float32 [8192], P('vocab')
The draws below stay inside these ranges and needn't reach their ends.
Inputs may be any that keep to these rules, and one draw needn't show every extreme that they name: `masked_pos`: each row lists 64 distinct positions of one sequence in increasing order; at most 8 of them fall in one aligned block of 256 positions, and exactly 8 in some blocks of every sequence. `t_num`: the two numerators differ.
All inputs are finite; a program needn't handle non-finite values.
Results may differ from the reference program's by a relative error of at most 0.0081.
Values may be sent and summed in bfloat16 or wider, within the bound.
A program may use at most 64 MiB of HBM per device.

```python
import math
import jax
import jax.numpy as jnp
import numpy as np
from jax import lax

D = 8192
TOK_DEV = 256
CAP = 8
VOC = 63232
TOKENS = 16384
LENGTH = 8192
KSEQ = 64


def loud_factor():
    return max(2.0, 80.0 / math.sqrt(D))


def loud_table(key):
    loud_count = max(VOC // 16, 2)
    order = jax.random.permutation(jax.random.fold_in(key, 13), VOC)
    is_loud = order < loud_count
    loud_list = jnp.argsort(order)[:loud_count].astype(jnp.int32)
    return (is_loud, loud_list)


def head_rows(key, row_ids):
    base_key = jax.random.fold_in(key, 11)
    is_loud, loud_list = loud_table(key)

    def draw_row(row_index):
        return jnp.clip(jax.random.normal(jax.random.fold_in(base_key, row_index), (D,), jnp.float32), -6.0, 6.0)
    scale_rows = jnp.where(is_loud[row_ids], loud_factor(), 1.0)[:, None]
    return jax.vmap(draw_row)(row_ids) * scale_rows * (4.0 / math.sqrt(D))


def draw_head(key, part):
    return head_rows(key, jnp.arange(VOC, dtype=jnp.int32)).astype(jnp.bfloat16)


def draw_t_num(key, part):
    num_key = jax.random.fold_in(key, 41)
    first_key, step_key = jax.random.split(num_key, 2)
    first = jax.random.randint(first_key, (), 1, 4)
    second = (first - 1 + jax.random.randint(step_key, (), 1, 3)) % 3 + 1
    return jnp.stack([first, second]).astype(jnp.int32)


def draw_hidden(key, part):
    hidden_key = jax.random.fold_in(key, 23)
    row_key = jax.random.fold_in(hidden_key, 0)
    col_key = jax.random.fold_in(hidden_key, 1)
    main_key = jax.random.fold_in(hidden_key, 2)
    pick_key = jax.random.fold_in(hidden_key, 4)
    mix_key = jax.random.fold_in(hidden_key, 5)
    gap_key = jax.random.fold_in(hidden_key, 6)
    amp_key = jax.random.fold_in(hidden_key, 7)
    row_amp = jnp.exp(jax.random.uniform(row_key, (TOKENS, 1), jnp.float32) * math.log(10.0))
    rising = jnp.exp(jnp.arange(D, dtype=jnp.float32) * (0.5 * math.log(3.0) / D))
    col_amp = jnp.exp(jax.random.uniform(col_key, (1, D), jnp.float32) * math.log(10.0)) * rising[None, :]
    values = jnp.clip(jax.random.normal(main_key, (TOKENS, D), jnp.float32), -3.0, 3.0) * row_amp * col_amp
    is_loud, loud_list = loud_table(key)
    loud_count = loud_list.shape[0]
    aligned = jnp.arange(0, TOKENS, 3, dtype=jnp.int32)
    count_aligned = aligned.shape[0]
    first_key, second_key, third_key = jax.random.split(pick_key, 3)
    first_slot = jax.random.randint(first_key, (count_aligned,), 0, loud_count)
    second_slot = (first_slot + jax.random.randint(second_key, (count_aligned,), 1, loud_count)) % loud_count
    third_slot = (first_slot + jax.random.randint(third_key, (count_aligned,), 1, loud_count)) % loud_count
    first = head_rows(key, loud_list[first_slot])
    second = head_rows(key, loud_list[second_slot])
    third = head_rows(key, loud_list[third_slot])
    mixing = jax.random.uniform(mix_key, (count_aligned, 1), jnp.float32)
    base_mix = first + second + mixing * third
    score_gap = jax.random.uniform(gap_key, (count_aligned,), jnp.float32, 1.5, 2.5)
    length_mix = jnp.sqrt(jnp.sum(base_mix * base_mix, axis=1))
    diff_mix = jnp.sum(base_mix * (first - second), axis=1)
    denominator = jnp.sum(first * (first - second), axis=1)
    along_first = (score_gap * length_mix / math.sqrt(D) - diff_mix) / denominator
    amplitude = jnp.exp(jax.random.uniform(amp_key, (count_aligned, 1), jnp.float32) * math.log(10.0))
    mixed_rows = (base_mix + along_first[:, None] * first) * (amplitude / loud_factor())
    values = values.at[aligned].set(mixed_rows)
    return values.astype(jnp.bfloat16)


def draw_one_sequence(seq_key):
    blocks = LENGTH // TOK_DEV
    hot_count = blocks // 8
    order_key, slot_key, place_key = jax.random.split(seq_key, 3)
    block_order = jax.random.permutation(order_key, blocks)
    is_hot = jnp.zeros((blocks,), jnp.bool_).at[block_order[:hot_count]].set(True)
    slot_score = jax.random.permutation(slot_key, blocks * CAP).reshape(blocks, CAP)
    slot_score = jnp.where(is_hot[:, None], slot_score + blocks * CAP, slot_score)
    slot_rank = jnp.argsort(jnp.argsort(slot_score.reshape(-1))).reshape(blocks, CAP)
    chosen = (slot_rank < KSEQ - hot_count * CAP).astype(jnp.int32)
    counts = jnp.where(is_hot, CAP, jnp.sum(chosen, axis=1))
    place_keys = jax.random.split(place_key, blocks)

    def block_places(block_key):
        return jax.random.permutation(block_key, TOK_DEV)
    places = jax.vmap(block_places)(place_keys)
    selected = (places < counts[:, None]).reshape(-1)
    return jnp.nonzero(selected, size=KSEQ)[0].astype(jnp.int32)


def draw_masked_pos(key, part):
    seq_keys = jax.random.split(jax.random.fold_in(key, 37), 2)
    return jax.vmap(draw_one_sequence)(seq_keys)


def touch_ends(result, key, low, largest):
    spot = [jax.random.randint(jax.random.fold_in(key, axis), (), 0, length) for axis, length in enumerate(result.shape)]
    main_axis = result.shape.index(max(result.shape))
    beside = spot[:main_axis] + [(spot[main_axis] + 1) % result.shape[main_axis]] + spot[main_axis + 1:]
    return result.at[tuple(spot)].set(low).at[tuple(beside)].set(largest)


def rank_bounds(amount, slope):
    weights = [(1 << 20) // math.isqrt(rank ** slope) + 1 for rank in range(1, amount + 1)]
    deviation = 1 + sum(weights) // (1 << 30)
    return np.cumsum(np.array([max(1, weight // deviation) for weight in weights]))


def skewed_ids(stream_key, extent, amount, slope):
    table = rank_bounds(amount, slope)
    pick = jax.random.randint(jax.random.fold_in(stream_key, 1), extent, 0, int(table[amount - 1]))
    grade = jnp.searchsorted(jnp.asarray(table, jnp.int32), pick, side="right")
    return jax.random.permutation(jax.random.fold_in(stream_key, 2), amount)[grade].astype(jnp.int32)


def setup_inputs(seed: int = 0) -> dict:
    splits = jax.random.split(jax.random.key(seed), 8)
    return {
        "hidden": draw_hidden(jax.random.fold_in(splits[7], 71), 0),
        "norm_gain": jnp.clip(1.0 + 0.1 * jax.random.normal(splits[1], (D,), jnp.float32), 0.5, 1.5),
        "head": draw_head(jax.random.fold_in(splits[7], 71), 0),
        "masked_pos": draw_masked_pos(jax.random.fold_in(splits[7], 71), 0),
        "masked_targets": touch_ends(skewed_ids(splits[4], (2, KSEQ), VOC, 2), jax.random.fold_in(splits[4], 3), 0, VOC - 1).astype(jnp.int32),
        "t_num": draw_t_num(jax.random.fold_in(splits[7], 71), 0),
        "t_den": jax.random.randint(splits[6], (2,), 192, 320).astype(jnp.int32),
    }


EPSILON = 1e-05
LOSS_SCALE = 1024.0

def reference(hidden, norm_gain, head, masked_pos, masked_targets, t_num, t_den):
    seq_base = (jnp.arange(2, dtype=jnp.int32) * LENGTH)[:, None]
    where_rows = (masked_pos + seq_base).reshape(-1).astype(jnp.int32)
    masked_rows = hidden[where_rows].astype(jnp.float32)
    inverse = lax.rsqrt(lax.optimization_barrier(jnp.mean(masked_rows * masked_rows, axis=1)) + EPSILON)
    normed = (masked_rows * inverse[:, None] * norm_gain[None, :]).astype(jnp.bfloat16)
    logits = lax.dot_general(normed, head, (((1,), (1,)), ((), ())), preferred_element_type=jnp.float32)
    row_top = lax.optimization_barrier(jnp.max(logits, axis=1, keepdims=True))
    exp_total = lax.optimization_barrier(jnp.sum(jnp.exp(logits - row_top), axis=1))
    log_total = row_top[:, 0] + jnp.log(exp_total)
    targets = masked_targets.reshape(-1).astype(jnp.int32)
    picked = jnp.take_along_axis(logits, targets[:, None], axis=1)[:, 0]
    weight = t_den.astype(jnp.float32) / (t_num.astype(jnp.float32) * (2.0 * LENGTH))
    factor = jnp.repeat(weight, KSEQ)
    loss_value = jnp.sum(factor * (log_total - picked))
    softmax_out = jnp.exp(logits - log_total[:, None])
    onehot = (jnp.arange(logits.shape[1], dtype=jnp.int32)[None, :] == targets[:, None]).astype(jnp.float32)
    dlogits = ((LOSS_SCALE * factor)[:, None] * (softmax_out - onehot)).astype(jnp.bfloat16)
    grad_head = lax.dot_general(dlogits, normed, (((0,), (0,)), ((), ())), preferred_element_type=jnp.float32).astype(jnp.bfloat16)
    dnormed = jnp.dot(dlogits, head, preferred_element_type=jnp.float32)
    grad_gain = lax.optimization_barrier(jnp.sum(dnormed * masked_rows * inverse[:, None], axis=0))
    inner_mean = lax.optimization_barrier(jnp.mean(norm_gain[None, :] * dnormed * masked_rows, axis=1))
    row_grads = inverse[:, None] * norm_gain[None, :] * dnormed - masked_rows * (inverse * inverse * inverse * inner_mean)[:, None]
    grad_hidden = jnp.zeros(hidden.shape, jnp.bfloat16).at[where_rows].set(row_grads.astype(jnp.bfloat16))
    return (loss_value, grad_hidden, grad_head, grad_gain)
```

```python
import jax
import jax.numpy as jnp
from jax import lax
from jax.experimental import pallas as pl
from jax.experimental.pallas import tpu as pltpu
from jax.sharding import PartitionSpec as P

MESH = pl.DeviceIdType.MESH
F32 = jnp.float32
BF16 = jnp.bfloat16
EPSILON = 1e-05
LOSS_SCALE = 1024.0
NX, NZ, NY = 4, 8, 8
ROWS = 128
SEQ_ROWS = 64
TOK = 256
WIDTH = 1024
MODEL = 8192
PADDED = 1024


def iota(shape, dim):
    return lax.broadcasted_iota(jnp.int32, shape, dim)


def column_of(lanes):
    n = lanes.shape[1]
    same = iota((n, n), 0) == iota((n, n), 1)
    return jnp.sum(jnp.where(same, lanes, 0.0), axis=1, keepdims=True)


def lanes_of(column):
    n = column.shape[0]
    same = iota((n, n), 0) == iota((n, n), 1)
    return jnp.sum(jnp.where(same, column, 0.0), axis=0, keepdims=True)


def combine(tiles):
    top = tiles[0][0:1]
    for t in tiles[1:]:
        top = jnp.maximum(top, t[0:1])
    total = weighted = picked = None
    for t in tiles:
        shift = t[0:1] - top
        scale = jnp.exp(shift)
        a = scale * t[1:2]
        b = scale * (t[2:3] + shift * t[1:2])
        c = t[3:4]
        total = a if total is None else total + a
        weighted = b if weighted is None else weighted + b
        picked = c if picked is None else picked + c
    return stack_rows(top, total, weighted, picked)


def stack_rows(*rows):
    sub = iota((8, ROWS), 0)
    out = jnp.zeros((8, ROWS), F32)
    for i, r in enumerate(rows):
        out = jnp.where(sub == i, r, out)
    return out


def main_kernel(
    hidden_hbm, gain_ref, head_hbm, pos_ref, tgt_ref, num_ref, den_ref,
    dl_out, normed_out, rg_out, gg_out, loss_out,
    hidden, head, slots, rows, lp, lrecv, e_all, cols,
    ss_y, ss_z, ss_x, ss_c, st_y, st_z, st_x, st_c,
    ubuf, crecv, xbuf, xrecv, zbuf, zrecv, rgall, ggz, ggx, ggc,
    load_sem,
    row_z_s, row_z_r, row_x_s, row_x_r, row_c_s, row_c_r,
    ss_s, ss_r, st_s, st_r, lg_s, lg_r, e_s, e_r,
    u_s, u_r, g_s, g_r, gg_s, gg_r,
):
    ctx = lax.axis_index("ctx")
    vy = lax.axis_index("vocab")
    x = ctx // 16
    z = (ctx // 2) % NZ
    k = ctx % 2
    voc = head.shape[0]

    def at_x(d):
        return (((x + d) % NX) * 16 + z * 2 + k, vy)

    def at_z(d):
        return (x * 16 + ((z + d) % NZ) * 2 + k, vy)

    def at_y(d):
        return (ctx, (vy + d) % NY)

    other = (x * 16 + z * 2 + (1 - k), vy)
    pair_d = 1 - 2 * (x % 2)
    pair = ((x + pair_d) * 16 + z * 2 + k, vy)

    load_hidden = pltpu.make_async_copy(hidden_hbm, hidden, load_sem.at[0])
    load_hidden.start()
    load_head = pltpu.make_async_copy(head_hbm, head, load_sem.at[1])
    load_head.start()

    barrier = pltpu.get_barrier_semaphore()
    peers = (
        [at_z(d) for d in range(1, NZ)]
        + [at_x(d) for d in range(1, NX)]
        + [at_y(d) for d in range(1, NY)]
        + [other]
    )
    for p in peers:
        pl.semaphore_signal(barrier, inc=1, device_id=p, device_id_type=MESH)

    def copy(src, dst, s, r, dev):
        return pltpu.make_async_remote_copy(
            src_ref=src, dst_ref=dst, send_sem=s, recv_sem=r, device_id=dev, device_id_type=MESH
        )

    sent = []

    def start(c):
        c.start()
        sent.append(c)
        return c

    pos = pos_ref[...].astype(F32)
    tgt = tgt_ref[...].astype(F32)
    pos_c = jnp.concatenate([column_of(pos[0:1]), column_of(pos[1:2]) + float(MODEL)], axis=0)
    tgt_c = jnp.concatenate([column_of(tgt[0:1]), column_of(tgt[1:2])], axis=0)
    cols[0] = jnp.broadcast_to(tgt_c, (ROWS, ROWS))
    pos_i = pos_c.astype(jnp.int32)
    owner_c = pos_i >> 8
    owner_l = lanes_of(owner_c.astype(F32))
    chosen = jnp.where(pos_i == ctx * TOK + iota((ROWS, TOK), 1), 1.0, 0.0)
    pick = jnp.sum(chosen.reshape(ROWS // 8, 8, TOK), axis=0).astype(BF16)
    load_hidden.wait()
    own = jnp.dot(pick, hidden[...], preferred_element_type=F32)
    half = WIDTH // 2
    slots[x, k, z] = jnp.concatenate([own[:, :half], own[:, half:]], axis=0).astype(BF16)
    squares = jnp.sum(own * own, axis=1, keepdims=True)
    lane8 = iota((8, ROWS), 1)
    mine = (lane8 % 8 == iota((8, ROWS), 0)) & (owner_l == ctx.astype(F32))
    ss = jnp.sum(jnp.where(mine, squares, 0.0), axis=0, keepdims=True)
    ss_y[vy] = jnp.broadcast_to(ss, (8, ROWS))

    pl.semaphore_wait(barrier, len(peers))

    def all_to_line(n, index, at, buf, ss_, rs_, base):
        cs = {}
        for d in range(1, n):
            cs[d] = start(copy(buf.at[index], buf.at[index], ss_.at[base + d], rs_.at[base + d], at(d)))
        return cs

    near = [1, 7, 2, 6, 3, 5, 4]
    cz = {}
    for d in [4, 3, 5, 2, 6, 1, 7]:
        cz[d] = start(copy(slots.at[x, k, z], slots.at[x, k, z], row_z_s.at[d], row_z_r.at[d], at_z(d)))
    cy = all_to_line(NY, vy, at_y, ss_y, ss_s, ss_r, 0)

    cx = {}

    def forward_x(d):
        zz = (z - d + NZ) % NZ
        for e in (2, 1, 3):
            cx[d, e] = start(
                copy(slots.at[x, k, zz], slots.at[x, k, zz], row_x_s.at[d, e], row_x_r.at[d, e], at_x(e))
            )

    forward_x(0)
    for d in near[:4]:
        cz[d].wait_recv()
        forward_x(d)
    for d in range(1, NY):
        cy[d].wait_recv()
    ss_z[z] = jnp.sum(ss_y[...], axis=0)
    cssz = all_to_line(NZ, z, at_z, ss_z, ss_s, ss_r, 8)
    for d in near[4:]:
        cz[d].wait_recv()
        forward_x(d)
    cc = {}

    def forward_core(e):
        xx = (x - e + NX) % NX
        cc[e] = start(copy(slots.at[xx, k], slots.at[xx, k], row_c_s.at[e], row_c_r.at[e], other))

    forward_core(0)
    for d in range(1, NZ):
        cssz[d].wait_recv()
    ss_x[x] = jnp.sum(ss_z[...], axis=0)
    cssx = all_to_line(NX, x, at_x, ss_x, ss_s, ss_r, 16)
    for e in (1, 3, 2):
        for d in range(NZ):
            cx[d, e].wait_recv()
        forward_core(e)
    for e in range(1, NX):
        cssx[e].wait_recv()
    ss_c[k] = jnp.sum(ss_x[...], axis=0)
    css = start(copy(ss_c.at[k], ss_c.at[k], ss_s.at[20], ss_r.at[20], other))
    for e in range(NX):
        cc[e].wait_recv()

    seq_block = owner_c - jnp.where(iota((ROWS, 1), 0) >= SEQ_ROWS, 32, 0)
    place = ((seq_block >> 4) * 16 + (seq_block & 1) * 8 + ((seq_block >> 1) & 7)) * 16 + (
        iota((ROWS, 1), 0) & 7
    )
    lane512 = iota((SEQ_ROWS, 512), 1)
    for s in range(2):
        here = place[s * SEQ_ROWS : (s + 1) * SEQ_ROWS]
        piece = slots[2 * s : 2 * s + 2].reshape(512, half)
        for h in range(2):
            spread = jnp.where(lane512 == here + 8 * h, 1.0, 0.0).astype(BF16)
            rows[s * SEQ_ROWS : (s + 1) * SEQ_ROWS, h * half : (h + 1) * half] = jnp.dot(
                spread, piece, preferred_element_type=F32
            )
    css.wait_recv()
    squares_l = (ss_c[0] + ss_c[1])[0:1]
    inv_l = lax.rsqrt(squares_l / float(MODEL) + EPSILON)
    inv_c = column_of(inv_l)
    cols[1] = jnp.broadcast_to(inv_c, (ROWS, ROWS))
    gain = gain_ref[...]
    normed = (rows[...] * inv_c * gain).astype(BF16)
    normed_out[...] = normed

    load_head.wait()
    lp[:, PADDED - 128 :] = jnp.zeros((ROWS, 128), F32)
    lp[:, :voc] = lax.dot_general(
        normed, head[...], (((1,), (1,)), ((), ())), preferred_element_type=F32
    )
    cl = {}
    for d in [4, 3, 5, 2, 6, 1, 7]:
        group = pl.ds(pl.multiple_of(((vy + d) % NY) * 16, 16), 16)
        cl[d] = start(copy(lp.at[group], lrecv.at[vy], lg_s.at[d], lg_r.at[d], at_y(d)))
    own_group = pl.ds(pl.multiple_of(vy * 16, 16), 16)
    lrecv[vy] = lp[own_group]
    for d in range(1, NY):
        cl[d].wait_recv()
    logits = lrecv[0]
    for i in range(1, NY):
        logits = logits + lrecv[i]

    lane = iota((16, PADDED), 1)
    live = lane < voc
    target = cols[0, own_group][:, 0:1].astype(jnp.int32) - ctx * voc
    top = jnp.max(jnp.where(live, logits, -jnp.inf), axis=1, keepdims=True)
    shifted = logits - top
    exps = jnp.where(live, jnp.exp(shifted), 0.0)
    e_all[own_group] = exps.astype(BF16)
    total = jnp.sum(exps, axis=1, keepdims=True)
    weighted = jnp.sum(exps * shifted, axis=1, keepdims=True)
    picked = jnp.sum(jnp.where(live & (lane == target), logits, 0.0), axis=1, keepdims=True)
    to_lane = iota((16, ROWS), 1) == vy * 16 + iota((16, ROWS), 0)
    st_y[vy] = stack_rows(
        *(jnp.sum(jnp.where(to_lane, v, 0.0), axis=0, keepdims=True) for v in (top, total, weighted, picked))
    )
    cy = all_to_line(NY, vy, at_y, st_y, st_s, st_r, 0)
    ce = {}
    for d in [4, 3, 5, 2, 6, 1, 7]:
        ce[d] = start(copy(e_all.at[own_group], e_all.at[own_group], e_s.at[d], e_r.at[d], at_y(d)))
    for d in range(1, NY):
        cy[d].wait_recv()
    block = jnp.sum(st_y[...], axis=0)
    st_z[z] = block
    cz = all_to_line(NZ, z, at_z, st_z, st_s, st_r, 8)
    for d in range(1, NZ):
        cz[d].wait_recv()
    st_x[x] = combine([st_z[i] for i in range(NZ)])
    cx = all_to_line(NX, x, at_x, st_x, st_s, st_r, 16)
    for d in range(1, NX):
        cx[d].wait_recv()
    st_c[k] = combine([st_x[i] for i in range(NX)])
    cst = start(copy(st_c.at[k], st_c.at[k], st_s.at[20], st_r.at[20], other))
    for d in range(1, NY):
        ce[d].wait_recv()
    cst.wait_recv()
    whole = combine([st_c[0], st_c[1]])

    lanes1 = iota((1, ROWS), 1)
    den = jnp.where(lanes1 < SEQ_ROWS, den_ref[0], den_ref[1]).astype(F32)
    num = jnp.where(lanes1 < SEQ_ROWS, num_ref[0], num_ref[1]).astype(F32)
    factor = den / (num * (2.0 * MODEL))
    log_total = whole[0:1] + jnp.log(whole[1:2])
    target_l = whole[3:4]
    loss = jnp.sum(factor * (log_total - target_l), axis=1, keepdims=True)
    loss_out[...] = jnp.broadcast_to(loss, (8, ROWS))
    scaled = LOSS_SCALE * factor
    w_c = column_of(scaled * jnp.exp(block[0:1] - log_total))
    t_c = column_of(scaled * (jnp.exp(target_l - log_total) - 1.0))
    inner = scaled * (whole[2:3] / whole[1:2] + (whole[0:1] - target_l)) / (inv_l * float(MODEL))
    cols[2] = jnp.broadcast_to(column_of(inv_l * inv_l * inv_l * inner), (ROWS, ROWS))
    is_target = iota((ROWS, PADDED), 1) + ctx * voc == tgt_c.astype(jnp.int32)
    is_target = is_target & (iota((ROWS, PADDED), 1) < voc)
    dl_out[...] = jnp.where(is_target, t_c, w_c * e_all[...].astype(F32)).astype(BF16)

    u = jnp.dot(dl_out[:, :voc], head[...], preferred_element_type=F32)
    for i in range(NX):
        for j in range(2):
            g = (i * 2 + j) * 16
            ubuf[j, i] = u[g : g + 16].astype(BF16)
    cu = start(copy(ubuf.at[1 - k], crecv, u_s.at[0], u_r.at[0], other))
    cu.wait_recv()
    xbuf[...] = (ubuf[k].astype(F32) + crecv[...].astype(F32)).astype(BF16)
    cu = {}
    for d in (2, 1, 3):
        cu[d] = start(copy(xbuf.at[(x + d) % NX], xrecv.at[x], u_s.at[d], u_r.at[d], at_x(d)))
    xrecv[x] = xbuf[x]
    for d in range(1, NX):
        cu[d].wait_recv()
    part = jnp.sum(xrecv[...].astype(F32), axis=0)
    for j in range(NZ):
        zbuf[j] = part[:, j * 128 : (j + 1) * 128].astype(BF16)
    cu = {}
    for d in [4, 3, 5, 2, 6, 1, 7]:
        cu[d] = start(copy(zbuf.at[(z + d) % NZ], zrecv.at[z], u_s.at[8 + d], u_r.at[8 + d], at_z(d)))
    zrecv[z] = zbuf[z]
    for d in range(1, NZ):
        cu[d].wait_recv()
    dn = jnp.sum(zrecv[...].astype(F32), axis=0)

    r0 = pl.ds(pl.multiple_of((x * 2 + k) * 16, 16), 16)
    c0 = pl.ds(pl.multiple_of(z * 128, 128), 128)
    rows_t = rows[r0, c0]
    inv_t = cols[1, r0]
    rg = inv_t * gain_ref[:, c0] * dn - rows_t * cols[2, r0]
    xl = x % 2
    rgall[k, xl, z] = rg.astype(BF16)
    ggz[z] = jnp.broadcast_to(jnp.sum(dn * rows_t * inv_t, axis=0, keepdims=True), (8, 128))
    cg = {}
    for d in [4, 3, 5, 2, 6, 1, 7]:
        cg[d] = start(copy(rgall.at[k, xl, z], rgall.at[k, xl, z], g_s.at[d], g_r.at[d], at_z(d)))
    cgg = all_to_line(NZ, z, at_z, ggz, gg_s, gg_r, 0)
    for d in range(1, NZ):
        cgg[d].wait_recv()
    sub = iota((8, 128), 0)
    gathered = jnp.zeros((8, 128), F32)
    for j in range(NZ):
        gathered = jnp.where(sub == j, ggz[j], gathered)
    ggx[x] = gathered
    cgg = all_to_line(NX, x, at_x, ggx, gg_s, gg_r, 8)
    for d in range(1, NZ):
        cg[d].wait_recv()
    cgx = start(copy(rgall.at[k, xl], rgall.at[k, xl], g_s.at[8], g_r.at[8], pair))
    for d in range(1, NX):
        cgg[d].wait_recv()
    ggc[k] = jnp.sum(ggx[...], axis=0)
    cgc = start(copy(ggc.at[k], ggc.at[k], gg_s.at[12], gg_r.at[12], other))
    cgx.wait_recv()
    cgr = start(copy(rgall.at[k], rgall.at[k], g_s.at[9], g_r.at[9], other))
    cgc.wait_recv()
    gg_out[...] = ggc[0] + ggc[1]
    cgr.wait_recv()
    for i in range(2):
        for j in range(2):
            g = (i * 2 + j) * 16
            for c in range(NZ):
                rg_out[g : g + 16, c * 128 : (c + 1) * 128] = rgall[j, i, c]
    for c in sent:
        c.wait_send()


def final_kernel(dl, normed, rg, pos_ref, gg, loss, gh_out, gx_out, gg_out, loss_out):
    ctx = lax.axis_index("ctx")
    voc = gh_out.shape[0]
    gh_out[...] = lax.dot_general(
        dl[:, :voc], normed[...], (((0,), (0,)), ((), ())), preferred_element_type=F32
    ).astype(BF16)
    pos = jnp.where(ctx < 32, pos_ref[0:1], pos_ref[1:2])
    local = pos - (ctx % 32) * TOK
    spread = jnp.where(iota((TOK, SEQ_ROWS), 0) == local, 1.0, 0.0).astype(BF16)
    gx_out[...] = jnp.dot(spread, rg[...], preferred_element_type=F32).astype(BF16)
    gg_out[...] = gg[...]
    loss_out[0, 0] = loss[0, 0]


def on_device(hidden, norm_gain, head, masked_pos, masked_targets, t_num, t_den):
    voc = head.shape[0]
    vm = pl.BlockSpec(memory_space=pltpu.VMEM)
    sm = pl.BlockSpec(memory_space=pltpu.SMEM)
    anyspace = pl.BlockSpec(memory_space=pl.ANY)
    V = pltpu.VMEM
    D = pltpu.SemaphoreType.DMA
    shape = jax.ShapeDtypeStruct
    dl, normed, rg, gg, loss = pl.pallas_call(
        main_kernel,
        name="main",
        out_shape=(
            shape((ROWS, PADDED), BF16),
            shape((ROWS, WIDTH), BF16),
            shape((SEQ_ROWS, WIDTH), BF16),
            shape((8, 128), F32),
            shape((8, 128), F32),
        ),
        in_specs=[anyspace, vm, anyspace, vm, vm, sm, sm],
        out_specs=(vm,) * 5,
        scratch_shapes=[
            V((TOK, WIDTH), BF16),
            V((voc, WIDTH), BF16),
            V((NX, 2, NZ, 16, WIDTH // 2), BF16),
            V((ROWS, WIDTH), F32),
            V((ROWS, PADDED), F32),
            V((NY, 16, PADDED), F32),
            V((ROWS, PADDED), BF16),
            V((3, ROWS, 128), F32),
            V((NY, 8, 128), F32),
            V((NZ, 8, 128), F32),
            V((NX, 8, 128), F32),
            V((2, 8, 128), F32),
            V((NY, 8, 128), F32),
            V((NZ, 8, 128), F32),
            V((NX, 8, 128), F32),
            V((2, 8, 128), F32),
            V((2, NX, 16, WIDTH), BF16),
            V((NX, 16, WIDTH), BF16),
            V((NX, 16, WIDTH), BF16),
            V((NX, 16, WIDTH), BF16),
            V((NZ, 16, 128), BF16),
            V((NZ, 16, 128), BF16),
            V((2, 2, NZ, 16, 128), BF16),
            V((NZ, 8, 128), F32),
            V((NX, 8, 128), F32),
            V((2, 8, 128), F32),
            D((2,)),
            D((8,)), D((8,)), D((8, 4)), D((8, 4)), D((4,)), D((4,)),
            D((24,)), D((24,)), D((24,)), D((24,)), D((8,)), D((8,)), D((8,)), D((8,)),
            D((16,)), D((16,)), D((16,)), D((16,)), D((16,)), D((16,)),
        ],
        compiler_params=pltpu.CompilerParams(
            collective_id=0, has_side_effects=True, vmem_limit_bytes=40 << 20
        ),
    )(hidden, norm_gain.reshape(1, WIDTH), head, masked_pos, masked_targets, t_num, t_den)
    grad_head, grad_hidden, grad_gain, loss_value = pl.pallas_call(
        final_kernel,
        name="final",
        out_shape=(
            shape((voc, WIDTH), BF16),
            shape((TOK, WIDTH), BF16),
            shape((8, 128), F32),
            shape((1, 1), F32),
        ),
        in_specs=[vm] * 6,
        out_specs=(vm, vm, vm, sm),
        compiler_params=pltpu.CompilerParams(vmem_limit_bytes=40 << 20),
    )(dl, normed, rg, masked_pos, gg, loss)
    return (loss_value.reshape(()), grad_hidden, grad_head, grad_gain.reshape(WIDTH))


def solution(mesh):
    placed = (P("ctx", "vocab"), P("vocab"), P("ctx", "vocab"), P(), P(), P(), P())
    return jax.shard_map(
        on_device,
        mesh=mesh,
        in_specs=placed,
        out_specs=(P(), P("ctx", "vocab"), P("ctx", "vocab"), P("vocab")),
        check_vma=False,
    )
```

```python
import jax
import jax.numpy as jnp
from jax import lax
from jax.experimental import pallas as pl
from jax.experimental.pallas import tpu as pltpu
from jax.sharding import PartitionSpec as P

MESH = pl.DeviceIdType.MESH
F32 = jnp.float32
BF16 = jnp.bfloat16
EPSILON = 1e-05
LOSS_SCALE = 1024.0
NX, NZ, NY = 4, 8, 8
ROWS = 128
SEQ_ROWS = 64
TOK = 256
WIDTH = 1024
MODEL = 8192
HALF = 512
FAR_FIRST = (4, 3, 5, 2, 6, 1, 7)
NEAR_FIRST = (1, 7, 2, 6, 3, 5, 4)


def iota(shape, dim):
    return lax.broadcasted_iota(jnp.int32, shape, dim)


def column_of(lanes):
    n = lanes.shape[1]
    same = iota((n, n), 0) == iota((n, n), 1)
    return jnp.sum(jnp.where(same, lanes, 0.0), axis=1, keepdims=True)


def lanes_of(column):
    n = column.shape[0]
    same = iota((n, n), 0) == iota((n, n), 1)
    return jnp.sum(jnp.where(same, column, 0.0), axis=0, keepdims=True)


def combine(tiles):
    top = tiles[0][0:1]
    for t in tiles[1:]:
        top = jnp.maximum(top, t[0:1])
    total = weighted = picked = None
    for t in tiles:
        shift = t[0:1] - top
        scale = jnp.exp(shift)
        a = scale * t[1:2]
        b = scale * (t[2:3] + shift * t[1:2])
        c = t[3:4]
        total = a if total is None else total + a
        weighted = b if weighted is None else weighted + b
        picked = c if picked is None else picked + c
    return stack_rows(top, total, weighted, picked)


def stack_rows(*rows):
    sub = iota((8, ROWS), 0)
    out = jnp.zeros((8, ROWS), F32)
    for i, r in enumerate(rows):
        out = jnp.where(sub == i, r, out)
    return out


def main_kernel(
    hidden_hbm, gain_hbm, head_hbm, pos_hbm, tgt_hbm, num_hbm, den_hbm,
    dlt_out, normed_out, rg_out, small_out,
    hidden, gain_ref, head, pos_ref, tgt_ref, num_ref, den_ref,
    slots, rows, lp, lrecv, e_all, cols,
    ss_y, ss_z, ss_x, ss_c, st_y, st_z, st_x, st_c,
    ubuf, crecv, xbuf, xrecv, zbuf, zrecv, tbuf, tcrecv, txbuf, txrecv, rgall, ggz, ggx, ggc,
    dlt, normed_v, small, load_sem,
    row_z_s, row_z_r, row_x_s, row_x_r, row_c_s, row_c_r,
    ss_s, ss_r, st_s, st_r, lg_s, lg_r, e_s, e_r,
    u_s, u_r, t_s, t_r, g_s, g_r, gg_s, gg_r,
):
    ctx = lax.axis_index("ctx")
    vy = lax.axis_index("vocab")
    x = ctx // 16
    z = (ctx // 2) % NZ
    k = ctx % 2
    voc = head.shape[0]

    def at_x(d):
        return (((x + d) % NX) * 16 + z * 2 + k, vy)

    def at_z(d):
        return (x * 16 + ((z + d) % NZ) * 2 + k, vy)

    def at_y(d):
        return (ctx, (vy + d) % NY)

    pair_x = x + 1 - 2 * (x % 2)

    def at_pair(d):
        return (pair_x * 16 + ((z + d) % NZ) * 2 + k, vy)

    other = (x * 16 + z * 2 + (1 - k), vy)

    loads = []
    for i, (a, b) in enumerate(
        (
            (pos_hbm, pos_ref), (hidden_hbm, hidden), (tgt_hbm, tgt_ref), (gain_hbm, gain_ref),
            (num_hbm, num_ref), (den_hbm, den_ref), (head_hbm, head),
        )
    ):
        loads.append(pltpu.make_async_copy(a, b, load_sem.at[i]))
        loads[-1].start()
    load_head = loads[-1]

    barrier = pltpu.get_barrier_semaphore()
    peers = (
        [at_z(d) for d in range(1, NZ)]
        + [at_x(d) for d in range(1, NX)]
        + [at_pair(d) for d in range(1, NZ)]
        + [at_y(d) for d in range(1, NY)]
        + [other]
    )
    for p in peers:
        pl.semaphore_signal(barrier, inc=1, device_id=p, device_id_type=MESH)

    def copy(src, dst, s, r, dev):
        return pltpu.make_async_remote_copy(
            src_ref=src, dst_ref=dst, send_sem=s, recv_sem=r, device_id=dev, device_id_type=MESH
        )

    sent = []

    def start(c):
        c.start()
        sent.append(c)
        return c

    def to_line(order, index, at, buf, ss_, rs_, base):
        return {d: start(copy(buf.at[index], buf.at[index], ss_.at[base + d], rs_.at[base + d], at(d))) for d in order}

    def keep(i, lanes):
        c = column_of(lanes)
        cols[i] = jnp.broadcast_to(c, (ROWS, 128))
        return c

    for c in loads[:-1]:
        c.wait()
    pos = pos_ref[...].astype(F32)
    tgt = tgt_ref[...].astype(F32)
    pos_c = jnp.concatenate([column_of(pos[0:1]), column_of(pos[1:2]) + float(MODEL)], axis=0)
    tgt_c = jnp.concatenate([column_of(tgt[0:1]), column_of(tgt[1:2])], axis=0)
    cols[0] = jnp.broadcast_to(tgt_c, (ROWS, 128))
    tgt_c = tgt_c.astype(jnp.int32)
    pos_i = pos_c.astype(jnp.int32)
    owner_c = pos_i >> 8
    owner_l = lanes_of(owner_c.astype(F32))
    chosen = jnp.where(pos_i == ctx * TOK + iota((ROWS, TOK), 1), 1.0, 0.0)
    pick = jnp.sum(chosen.reshape(ROWS // 8, 8, TOK), axis=0).astype(BF16)
    own = jnp.dot(pick, hidden[...], preferred_element_type=F32)
    half = WIDTH // 2
    slots[x, k, z] = jnp.concatenate([own[:, :half], own[:, half:]], axis=0).astype(BF16)
    squares = jnp.sum(own * own, axis=1, keepdims=True)
    lane8 = iota((8, ROWS), 1)
    mine = (lane8 % 8 == iota((8, ROWS), 0)) & (owner_l == ctx.astype(F32))
    ss = jnp.sum(jnp.where(mine, squares, 0.0), axis=0, keepdims=True)
    ss_y[vy] = jnp.broadcast_to(ss, (8, ROWS))

    pl.semaphore_wait(barrier, len(peers))

    cz = to_line(FAR_FIRST, (x, k, z), at_z, slots, row_z_s, row_z_r, 0)
    cy = to_line(FAR_FIRST, vy, at_y, ss_y, ss_s, ss_r, 0)
    cx = {}

    def forward_x(d):
        zz = (z - d + NZ) % NZ
        for e in (2, 1, 3):
            cx[d, e] = start(
                copy(slots.at[x, k, zz], slots.at[x, k, zz], row_x_s.at[d, e], row_x_r.at[d, e], at_x(e))
            )

    forward_x(0)
    for d in NEAR_FIRST[:4]:
        cz[d].wait_recv()
        forward_x(d)
    for d in range(1, NY):
        cy[d].wait_recv()
    ss_z[z] = jnp.sum(ss_y[...], axis=0)
    cssz = to_line(FAR_FIRST, z, at_z, ss_z, ss_s, ss_r, 8)
    for d in NEAR_FIRST[4:]:
        cz[d].wait_recv()
        forward_x(d)
    cc = {}

    def forward_core(e):
        xx = (x - e + NX) % NX
        cc[e] = start(copy(slots.at[xx, k], slots.at[xx, k], row_c_s.at[e], row_c_r.at[e], other))

    forward_core(0)
    for d in range(1, NZ):
        cssz[d].wait_recv()
    ss_x[x] = jnp.sum(ss_z[...], axis=0)
    cssx = to_line((2, 1, 3), x, at_x, ss_x, ss_s, ss_r, 16)
    for e in (1, 3, 2):
        for d in range(NZ):
            cx[d, e].wait_recv()
        forward_core(e)
    for e in range(1, NX):
        cssx[e].wait_recv()
    ss_c[k] = jnp.sum(ss_x[...], axis=0)
    css = start(copy(ss_c.at[k], ss_c.at[k], ss_s.at[20], ss_r.at[20], other))
    for e in range(NX):
        cc[e].wait_recv()

    seq_block = owner_c - jnp.where(iota((ROWS, 1), 0) >= SEQ_ROWS, 32, 0)
    place = ((seq_block >> 4) * 16 + (seq_block & 1) * 8 + ((seq_block >> 1) & 7)) * 16 + (
        iota((ROWS, 1), 0) & 7
    )
    lane512 = iota((SEQ_ROWS, 512), 1)
    for s in range(2):
        here = place[s * SEQ_ROWS : (s + 1) * SEQ_ROWS]
        piece = slots[2 * s : 2 * s + 2].reshape(512, half)
        for h in range(2):
            spread = jnp.where(lane512 == here + 8 * h, 1.0, 0.0).astype(BF16)
            rows[s * SEQ_ROWS : (s + 1) * SEQ_ROWS, h * half : (h + 1) * half] = jnp.dot(
                spread, piece, preferred_element_type=F32
            )
    css.wait_recv()
    squares_l = (ss_c[0] + ss_c[1])[0:1]
    inv_l = lax.rsqrt(squares_l / float(MODEL) + EPSILON)
    inv_c = keep(1, inv_l)
    normed = (rows[...] * inv_c * gain_ref[...]).astype(BF16)
    normed_v[...] = normed
    stores = []

    def store(i, a, b):
        stores.append(pltpu.make_async_copy(a, b, load_sem.at[i]))
        stores[-1].start()

    store(0, normed_v, normed_out)

    load_head.wait()
    lives = (HALF, voc - HALF)
    head_part = (head.at[0:HALF], head.at[HALF:voc])
    own_group = pl.ds(pl.multiple_of(vy * 16, 16), 16)
    lp[1, :, HALF - 128 :] = jnp.zeros((ROWS, 128), F32)
    cl = {}
    for h in range(2):
        lp[h, :, : lives[h]] = lax.dot_general(
            normed, head_part[h][...], (((1,), (1,)), ((), ())), preferred_element_type=F32
        )
        for d in FAR_FIRST:
            group = pl.ds(pl.multiple_of(((vy + d) % NY) * 16, 16), 16)
            cl[h, d] = start(
                copy(lp.at[h, group], lrecv.at[h, vy], lg_s.at[8 * h + d], lg_r.at[8 * h + d], at_y(d))
            )
        lrecv[h, vy] = lp[h, own_group]

    is_target = []
    for h in range(2):
        entry = iota((ROWS, HALF), 1) + h * HALF
        is_target.append((entry + ctx * voc == tgt_c) & (entry < voc))

    def over_vocab(left):
        return sum(
            jnp.dot(left[h][:, : lives[h]], head_part[h][...], preferred_element_type=F32)
            for h in range(2)
        )

    def split(value, buf):
        for i in range(NX):
            for j in range(2):
                g = (i * 2 + j) * 16
                buf[j, i] = value[g : g + 16].astype(BF16)

    split(over_vocab([jnp.where(t, 1.0, 0.0).astype(BF16) for t in is_target]), tbuf)
    ct = start(copy(tbuf.at[1 - k], tcrecv, t_s.at[0], t_r.at[0], other))
    ct.wait_recv()
    txbuf[...] = (tbuf[k].astype(F32) + tcrecv[...].astype(F32)).astype(BF16)
    ct = {
        d: start(copy(txbuf.at[(x + d) % NX], txrecv.at[x], t_s.at[d], t_r.at[d], at_x(d)))
        for d in (2, 1, 3)
    }
    txrecv[x] = txbuf[x]

    to_lane = iota((16, ROWS), 1) == vy * 16 + iota((16, ROWS), 0)
    target16 = cols[0, own_group][:, 0:1].astype(jnp.int32) - ctx * voc
    stat_rows = []
    ce = {}
    for h in range(2):
        for d in range(1, NY):
            cl[h, d].wait_recv()
        logits = lrecv[h, 0]
        for i in range(1, NY):
            logits = logits + lrecv[h, i]
        lane = iota((16, HALF), 1)
        live = lane < lives[h]
        top = jnp.max(jnp.where(live, logits, -jnp.inf), axis=1, keepdims=True)
        shifted = logits - top
        exps = jnp.where(live, jnp.exp(shifted), 0.0)
        e_all[h, own_group] = exps.astype(BF16)
        stat = (
            top,
            jnp.sum(exps, axis=1, keepdims=True),
            jnp.sum(exps * shifted, axis=1, keepdims=True),
            jnp.sum(jnp.where(live & (lane + h * HALF == target16), logits, 0.0), axis=1, keepdims=True),
        )
        stat_rows += [jnp.sum(jnp.where(to_lane, v, 0.0), axis=0, keepdims=True) for v in stat]
        if h == 1:
            st_y[vy] = stack_rows(*stat_rows)
            cy = to_line(FAR_FIRST, vy, at_y, st_y, st_s, st_r, 0)
        for d in FAR_FIRST:
            ce[h, d] = start(
                copy(
                    e_all.at[h, own_group], e_all.at[h, own_group],
                    e_s.at[8 * h + d], e_r.at[8 * h + d], at_y(d),
                )
            )

    for d in range(1, NY):
        cy[d].wait_recv()
    block = jnp.sum(st_y[...], axis=0)
    tops = (block[0:1], block[4:5])
    st_c[k] = combine([block[0:4], block[4:8]])
    cst = start(copy(st_c.at[k], st_c.at[k], st_s.at[20], st_r.at[20], other))
    cst.wait_recv()
    by_core = combine([st_c[0], st_c[1]])
    st_x[x] = by_core
    cx = to_line((2, 1, 3), x, at_x, st_x, st_s, st_r, 16)

    u = None
    for h in range(2):
        scale = column_of(jnp.exp(tops[h] - by_core[0:1]))
        for d in range(1, NY):
            ce[h, d].wait_recv()
        left = jnp.where(is_target[h], 0.0, scale * e_all[h].astype(F32)).astype(BF16)
        part = jnp.dot(left[:, : lives[h]], head_part[h][...], preferred_element_type=F32)
        u = part if u is None else u + part
    split(u, ubuf)
    cu = start(copy(ubuf.at[1 - k], crecv, u_s.at[0], u_r.at[0], other))
    for d in range(1, NX):
        cx[d].wait_recv()
    by_x = combine([st_x[i] for i in range(NX)])
    st_z[z] = by_x
    cz = to_line(FAR_FIRST, z, at_z, st_z, st_s, st_r, 8)
    keep(3, jnp.exp(by_core[0:1] - by_x[0:1]))
    cu.wait_recv()
    for i in range(NX):
        scale = cols[3, pl.ds(pl.multiple_of((2 * i + k) * 16, 16), 16)][:, 0:1]
        xbuf[i] = (scale * (ubuf[k, i].astype(F32) + crecv[i].astype(F32))).astype(BF16)
    cu = {
        d: start(copy(xbuf.at[(x + d) % NX], xrecv.at[x], u_s.at[d], u_r.at[d], at_x(d)))
        for d in (2, 1, 3)
    }
    xrecv[x] = xbuf[x]
    for d in range(1, NZ):
        cz[d].wait_recv()
    whole = combine([st_z[i] for i in range(NZ)])

    lanes1 = iota((1, ROWS), 1)
    den = jnp.where(lanes1 < SEQ_ROWS, den_ref[0], den_ref[1]).astype(F32)
    num = jnp.where(lanes1 < SEQ_ROWS, num_ref[0], num_ref[1]).astype(F32)
    factor = den / (num * (2.0 * MODEL))
    log_total = whole[0:1] + jnp.log(whole[1:2])
    target_l = whole[3:4]
    scaled = LOSS_SCALE * factor
    t_c = keep(5, scaled * (jnp.exp(target_l - log_total) - 1.0))
    keep(4, scaled * jnp.exp(by_x[0:1] - log_total))
    r0 = pl.ds(pl.multiple_of((x * 2 + k) * 16, 16), 16)
    c0 = pl.ds(pl.multiple_of(z * 128, 128), 128)
    for d in range(1, NX):
        ct[d].wait_recv()
    of_targets = cols[5, r0][:, 0:1] * jnp.sum(txrecv[...].astype(F32), axis=0)
    for d in range(1, NX):
        cu[d].wait_recv()
    part = cols[4, r0][:, 0:1] * jnp.sum(xrecv[...].astype(F32), axis=0) + of_targets
    for j in range(NZ):
        zbuf[j] = part[:, j * 128 : (j + 1) * 128].astype(BF16)
    cu = {
        d: start(copy(zbuf.at[(z + d) % NZ], zrecv.at[z], u_s.at[8 + d], u_r.at[8 + d], at_z(d)))
        for d in FAR_FIRST
    }
    zrecv[z] = zbuf[z]
    gain_part = jnp.sum(part * rows[r0, :] * cols[1, r0][:, 0:1], axis=0, keepdims=True)
    ggz[z] = stack_rows(*(gain_part[:, j * 128 : (j + 1) * 128] for j in range(NZ)))
    cgg = to_line(FAR_FIRST, z, at_z, ggz, gg_s, gg_r, 0)

    loss = jnp.sum(factor * (log_total - target_l), axis=1, keepdims=True)
    small[8:16] = jnp.broadcast_to(loss, (8, ROWS))
    inner = scaled * (whole[2:3] / whole[1:2] + (whole[0:1] - target_l)) / (inv_l * float(MODEL))
    keep(2, inv_l * inv_l * inv_l * inner)
    for d in range(1, NZ):
        cu[d].wait_recv()
    dn = jnp.sum(zrecv[...].astype(F32), axis=0)
    rg = cols[1, r0] * gain_ref[:, c0] * dn - rows[r0, c0] * cols[2, r0]
    xl = x % 2
    rgall[xl, k, z] = rg.astype(BF16)
    mine = rgall.at[xl, k, z]
    cg = {}
    for d in FAR_FIRST:
        cg[d] = start(copy(mine, mine, g_s.at[d], g_r.at[d], at_z(d)))
    for d in FAR_FIRST + (0,):
        cg[8 + d] = start(copy(mine, mine, g_s.at[8 + d], g_r.at[8 + d], at_pair(d)))
    for d in range(1, NZ):
        cgg[d].wait_recv()
    ggx[x] = jnp.sum(ggz[...], axis=0)
    cgg = to_line((2, 1, 3), x, at_x, ggx, gg_s, gg_r, 8)
    for h in range(2):
        w_c = column_of(scaled * jnp.exp(tops[h] - log_total))
        dl = jnp.where(is_target[h], t_c, w_c * e_all[h].astype(F32))
        dlt[h * HALF : (h + 1) * HALF] = dl.T.astype(BF16)
    store(1, dlt, dlt_out)
    for d in range(1, NX):
        cgg[d].wait_recv()
    ggc[k] = jnp.sum(ggx[...], axis=0)
    cgc = start(copy(ggc.at[k], ggc.at[k], gg_s.at[12], gg_r.at[12], other))
    for c in cg.values():
        c.wait_recv()
    cgr = start(copy(rgall.at[:, k], rgall.at[:, k], g_s.at[16], g_r.at[16], other))
    cgc.wait_recv()
    small[0:8] = ggc[0] + ggc[1]
    store(2, small, small_out)
    for c in sent[:-1]:
        c.wait_send()
    cgr.wait_recv()
    store(3, rgall, rg_out)
    cgr.wait_send()
    for c in stores:
        c.wait()


def final_kernel(
    dlt_hbm, normed_hbm, rg_hbm, small_hbm, pos_hbm, gh_out, gx_out, gg_out, loss_out,
    dlt, normed, rg, small, pos_ref, gh, gx, sems,
):
    loads = []
    for i, (a, b) in enumerate(
        ((dlt_hbm, dlt), (normed_hbm, normed), (pos_hbm, pos_ref), (rg_hbm, rg), (small_hbm, small))
    ):
        loads.append(pltpu.make_async_copy(a, b, sems.at[i]))
        loads[-1].start()
    ctx = lax.axis_index("ctx")
    voc = gh.shape[0]
    for c in loads[:2]:
        c.wait()
    stores = []
    step = WIDTH // 4
    for i in range(4):
        c = slice(i * step, (i + 1) * step)
        gh[:, c] = jnp.dot(dlt[:voc], normed[:, c], preferred_element_type=F32).astype(BF16)
        stores.append(pltpu.make_async_copy(gh.at[:, c], gh_out.at[:, c], sems.at[8 + i]))
        stores[-1].start()
    for c in loads[2:]:
        c.wait()
    pos = jnp.where(ctx < 32, pos_ref[0:1], pos_ref[1:2])
    local = pos - (ctx % 32) * TOK
    spread = jnp.where(iota((TOK, SEQ_ROWS), 0) == local, 1.0, 0.0).astype(BF16)
    for j in range(NZ):
        piece = rg[:, :, j].reshape(SEQ_ROWS, 128)
        gx[:, j * 128 : (j + 1) * 128] = jnp.dot(spread, piece, preferred_element_type=F32).astype(BF16)
    stores.append(pltpu.make_async_copy(gx, gx_out, sems.at[5]))
    stores[-1].start()
    stores.append(pltpu.make_async_copy(small.at[0:8], gg_out, sems.at[6]))
    stores[-1].start()
    loss_out[0, 0] = small[8, 0]
    for c in stores:
        c.wait()


def on_device(hidden, norm_gain, head, masked_pos, masked_targets, t_num, t_den):
    voc = head.shape[0]
    sm = pl.BlockSpec(memory_space=pltpu.SMEM)
    hbm = pl.BlockSpec(memory_space=pltpu.HBM)
    V = pltpu.VMEM
    D = pltpu.SemaphoreType.DMA
    S = pltpu.SMEM
    I32 = jnp.int32
    shape = jax.ShapeDtypeStruct
    dlt, normed, rg, small = pl.pallas_call(
        main_kernel,
        name="main",
        out_shape=(
            shape((2 * HALF, ROWS), BF16),
            shape((ROWS, WIDTH), BF16),
            shape((2, 2, NZ, 16, 128), BF16),
            shape((16, 128), F32),
        ),
        in_specs=[hbm] * 7,
        out_specs=(hbm,) * 4,
        scratch_shapes=[
            V((TOK, WIDTH), BF16), V((1, WIDTH), F32), V((voc, WIDTH), BF16),
            V((2, SEQ_ROWS), I32), V((2, SEQ_ROWS), I32), S((2,), I32), S((2,), I32),
            V((NX, 2, NZ, 16, WIDTH // 2), BF16),
            V((ROWS, WIDTH), F32),
            V((2, ROWS, HALF), F32),
            V((2, NY, 16, HALF), F32),
            V((2, ROWS, HALF), BF16),
            V((6, ROWS, 128), F32),
            V((NY, 8, 128), F32), V((NZ, 8, 128), F32), V((NX, 8, 128), F32), V((2, 8, 128), F32),
            V((NY, 8, 128), F32), V((NZ, 8, 128), F32), V((NX, 8, 128), F32), V((2, 8, 128), F32),
            V((2, NX, 16, WIDTH), BF16), V((NX, 16, WIDTH), BF16),
            V((NX, 16, WIDTH), BF16), V((NX, 16, WIDTH), BF16),
            V((NZ, 16, 128), BF16), V((NZ, 16, 128), BF16),
            V((2, NX, 16, WIDTH), BF16), V((NX, 16, WIDTH), BF16),
            V((NX, 16, WIDTH), BF16), V((NX, 16, WIDTH), BF16),
            V((2, 2, NZ, 16, 128), BF16),
            V((NZ, 8, 128), F32), V((NX, 8, 128), F32), V((2, 8, 128), F32),
            V((2 * HALF, ROWS), BF16), V((ROWS, WIDTH), BF16), V((16, 128), F32),
            D((8,)),
            D((8,)), D((8,)), D((8, 4)), D((8, 4)), D((4,)), D((4,)),
            D((24,)), D((24,)), D((24,)), D((24,)), D((16,)), D((16,)), D((16,)), D((16,)),
            D((16,)), D((16,)), D((4,)), D((4,)), D((17,)), D((17,)), D((16,)), D((16,)),
        ],
        compiler_params=pltpu.CompilerParams(
            collective_id=0, has_side_effects=True, vmem_limit_bytes=60 << 20
        ),
    )(hidden, norm_gain.reshape(1, WIDTH), head, masked_pos, masked_targets, t_num, t_den)
    grad_head, grad_hidden, grad_gain, loss_value = pl.pallas_call(
        final_kernel,
        name="final",
        out_shape=(
            shape((voc, WIDTH), BF16),
            shape((TOK, WIDTH), BF16),
            shape((8, 128), F32),
            shape((1, 1), F32),
        ),
        in_specs=[hbm] * 5,
        out_specs=(hbm, hbm, hbm, sm),
        scratch_shapes=[
            V((2 * HALF, ROWS), BF16), V((ROWS, WIDTH), BF16), V((2, 2, NZ, 16, 128), BF16),
            V((16, 128), F32), V((2, SEQ_ROWS), I32),
            V((voc, WIDTH), BF16), V((TOK, WIDTH), BF16), D((12,)),
        ],
        compiler_params=pltpu.CompilerParams(vmem_limit_bytes=60 << 20),
    )(dlt, normed, rg, small, masked_pos)
    return (loss_value.reshape(()), grad_hidden, grad_head, grad_gain.reshape(WIDTH))


def solution(mesh):
    placed = (P("ctx", "vocab"), P("vocab"), P("ctx", "vocab"), P(), P(), P(), P())
    return jax.shard_map(
        on_device,
        mesh=mesh,
        in_specs=placed,
        out_specs=(P(), P("ctx", "vocab"), P("ctx", "vocab"), P("vocab")),
        check_vma=False,
    )
```

```python
import jax
import jax.numpy as jnp
from jax import lax
from jax.experimental import pallas as pl
from jax.experimental.pallas import tpu as pltpu
from jax.sharding import PartitionSpec as P

MESH = pl.DeviceIdType.MESH
F32 = jnp.float32
BF16 = jnp.bfloat16
EPSILON = 1e-05
LOSS_SCALE = 1024.0
NX, NZ, NY = 4, 8, 8
ROWS = 128
SEQ_ROWS = 64
TOK = 256
WIDTH = 1024
MODEL = 8192
HALF = 512
FAR_FIRST = (4, 3, 5, 2, 6, 1, 7)
NEAR_FIRST = (1, 7, 2, 6, 3, 5, 4)


def iota(shape, dim):
    return lax.broadcasted_iota(jnp.int32, shape, dim)


def column_of(lanes):
    n = lanes.shape[1]
    same = iota((n, n), 0) == iota((n, n), 1)
    return jnp.sum(jnp.where(same, lanes, 0.0), axis=1, keepdims=True)


def columns(*lanes):
    turned = stack_rows(*lanes).T
    return [turned[:, i : i + 1] for i in range(len(lanes))]


def rows16(lanes, start):
    same = iota((16, ROWS), 1) == start + iota((16, ROWS), 0)
    return jnp.sum(jnp.where(same, lanes, 0.0), axis=1, keepdims=True)


def lanes_of(column):
    n = column.shape[0]
    same = iota((n, n), 0) == iota((n, n), 1)
    return jnp.sum(jnp.where(same, column, 0.0), axis=0, keepdims=True)


def combine(tiles):
    top = tiles[0][0:1]
    for t in tiles[1:]:
        top = jnp.maximum(top, t[0:1])
    total = weighted = picked = None
    for t in tiles:
        shift = t[0:1] - top
        scale = jnp.exp(shift)
        a = scale * t[1:2]
        b = scale * (t[2:3] + shift * t[1:2])
        c = t[3:4]
        total = a if total is None else total + a
        weighted = b if weighted is None else weighted + b
        picked = c if picked is None else picked + c
    return stack_rows(top, total, weighted, picked)


def stack_rows(*rows):
    sub = iota((8, ROWS), 0)
    out = jnp.zeros((8, ROWS), F32)
    for i, r in enumerate(rows):
        out = jnp.where(sub == i, r, out)
    return out


def main_kernel(
    hidden_hbm, gain_hbm, head_hbm, pos_hbm, tgt_hbm, num_hbm, den_hbm,
    dlt_out, normed_out, rg_out, small_out,
    hidden, gain_ref, head, pos_ref, tgt_ref, num_ref, den_ref,
    slots, rows, lp, relay, relay4, lrecv, e_all,
    ss_y, ss_p, ss_c, st_y, st_z, st_x, st_c,
    ubuf, crecv, xbuf, xrecv, zbuf, zrecv, tbuf, tcrecv, txbuf, txrecv, tzbuf, tzrecv, rgall, gg_p, ggc,
    dlt, normed_v, small, load_sem,
    row_z_s, row_z_r, row_x_s, row_x_r, row_c_s, row_c_r,
    ss_s, ss_r, ssp_s, ssp_r, st_s, st_r, rl_s, rl_r, lg_s, lg_r, e_s, e_r,
    u_s, u_r, t_s, t_r, g_s, g_r, gg_s, gg_r, ggp_s, ggp_r,
):
    ctx = lax.axis_index("ctx")
    vy = lax.axis_index("vocab")
    x = ctx // 16
    z = (ctx // 2) % NZ
    k = ctx % 2
    voc = head.shape[0]

    def at_x(d):
        return (((x + d) % NX) * 16 + z * 2 + k, vy)

    def at_z(d):
        return (x * 16 + ((z + d) % NZ) * 2 + k, vy)

    def at_y(d):
        return (ctx, (vy + d) % NY)

    pair_x = x + 1 - 2 * (x % 2)

    def at_pair(d):
        return (pair_x * 16 + ((z + d) % NZ) * 2 + k, vy)

    def at_xz(e, d):
        return (((x + e) % NX) * 16 + ((z + d) % NZ) * 2 + k, vy)

    plane = [(e, d) for d in FAR_FIRST + (0,) for e in (2, 1, 3, 0) if (e, d) != (0, 0)]
    other = (x * 16 + z * 2 + (1 - k), vy)

    loads = []
    for i, (a, b) in enumerate(
        (
            (pos_hbm, pos_ref), (hidden_hbm, hidden), (tgt_hbm, tgt_ref), (gain_hbm, gain_ref),
            (num_hbm, num_ref), (den_hbm, den_ref), (head_hbm, head),
        )
    ):
        loads.append(pltpu.make_async_copy(a, b, load_sem.at[i]))
        loads[-1].start()
    load_head = loads[-1]

    barrier = pltpu.get_barrier_semaphore()
    peers = [at_xz(e, d) for e, d in plane] + [at_y(d) for d in range(1, NY)] + [other]
    for p in peers:
        pl.semaphore_signal(barrier, inc=1, device_id=p, device_id_type=MESH)

    def copy(src, dst, s, r, dev):
        return pltpu.make_async_remote_copy(
            src_ref=src, dst_ref=dst, send_sem=s, recv_sem=r, device_id=dev, device_id_type=MESH
        )

    sent = []

    def start(c):
        c.start()
        sent.append(c)
        return c

    def to_line(order, index, at, buf, ss_, rs_, base):
        return {d: start(copy(buf.at[index], buf.at[index], ss_.at[base + d], rs_.at[base + d], at(d))) for d in order}

    def to_plane(buf, ss_, rs_):
        mine = buf.at[x, z]
        return [start(copy(mine, mine, ss_.at[e, d], rs_.at[e, d], at_xz(e, d))) for e, d in plane]

    for c in loads[:-1]:
        c.wait()
    pos = pos_ref[...].astype(F32)
    tgt = tgt_ref[...].astype(F32)
    pos_c = jnp.concatenate([column_of(pos[0:1]), column_of(pos[1:2]) + float(MODEL)], axis=0)
    tgt_c = jnp.concatenate([column_of(tgt[0:1]), column_of(tgt[1:2])], axis=0)
    tgt_l = lanes_of(tgt_c)
    tgt_c = tgt_c.astype(jnp.int32)
    pos_i = pos_c.astype(jnp.int32)
    owner_c = pos_i >> 8
    owner_l = lanes_of(owner_c.astype(F32))
    chosen = jnp.where(pos_i == ctx * TOK + iota((ROWS, TOK), 1), 1.0, 0.0)
    pick = jnp.sum(chosen.reshape(ROWS // 8, 8, TOK), axis=0).astype(BF16)
    own = jnp.dot(pick, hidden[...], preferred_element_type=F32)
    half = WIDTH // 2
    slots[x, k, z] = jnp.concatenate([own[:, :half], own[:, half:]], axis=0).astype(BF16)
    squares = jnp.sum(own * own, axis=1, keepdims=True)
    lane8 = iota((8, ROWS), 1)
    mine = (lane8 % 8 == iota((8, ROWS), 0)) & (owner_l == ctx.astype(F32))
    ss = jnp.sum(jnp.where(mine, squares, 0.0), axis=0, keepdims=True)
    ss_y[vy] = ss

    pl.semaphore_wait(barrier, len(peers))

    cz = to_line(FAR_FIRST, (x, k, z), at_z, slots, row_z_s, row_z_r, 0)
    cy = to_line(FAR_FIRST, vy, at_y, ss_y, ss_s, ss_r, 0)
    cx = {}

    def forward_x(d):
        zz = (z - d + NZ) % NZ
        for e in (2, 1, 3):
            cx[d, e] = start(
                copy(slots.at[x, k, zz], slots.at[x, k, zz], row_x_s.at[d, e], row_x_r.at[d, e], at_x(e))
            )

    forward_x(0)
    for d in NEAR_FIRST[:4]:
        cz[d].wait_recv()
        forward_x(d)
    for d in range(1, NY):
        cy[d].wait_recv()
    ss_p[x, z] = jnp.sum(ss_y[...], axis=0)
    cssp = to_plane(ss_p, ssp_s, ssp_r)
    for d in NEAR_FIRST[4:]:
        cz[d].wait_recv()
        forward_x(d)
    cc = {}

    def forward_core(e):
        xx = (x - e + NX) % NX
        cc[e] = start(copy(slots.at[xx, k], slots.at[xx, k], row_c_s.at[e], row_c_r.at[e], other))

    forward_core(0)
    for e in (1, 3, 2):
        for d in range(NZ):
            cx[d, e].wait_recv()
        forward_core(e)
    for c in cssp:
        c.wait_recv()
    ss_c[k] = jnp.sum(ss_p[...].reshape(NX * NZ, 1, ROWS), axis=0)
    css = start(copy(ss_c.at[k], ss_c.at[k], ss_s.at[20], ss_r.at[20], other))
    for e in range(NX):
        cc[e].wait_recv()

    seq_block = owner_c - jnp.where(iota((ROWS, 1), 0) >= SEQ_ROWS, 32, 0)
    place = ((seq_block >> 4) * 16 + (seq_block & 1) * 8 + ((seq_block >> 1) & 7)) * 16 + (
        iota((ROWS, 1), 0) & 7
    )
    lane512 = iota((SEQ_ROWS, 512), 1)
    for s in range(2):
        here = place[s * SEQ_ROWS : (s + 1) * SEQ_ROWS]
        piece = slots[2 * s : 2 * s + 2].reshape(512, half)
        for h in range(2):
            spread = jnp.where(lane512 == here + 8 * h, 1.0, 0.0).astype(BF16)
            rows[s * SEQ_ROWS : (s + 1) * SEQ_ROWS, h * half : (h + 1) * half] = jnp.dot(
                spread, piece, preferred_element_type=F32
            )
    css.wait_recv()
    squares_l = ss_c[0] + ss_c[1]
    inv_l = lax.rsqrt(squares_l / float(MODEL) + EPSILON)
    [inv_c] = columns(inv_l)
    normed = (rows[...] * inv_c * gain_ref[...]).astype(BF16)
    normed_v[...] = normed
    stores = []

    def store(i, a, b):
        stores.append(pltpu.make_async_copy(a, b, load_sem.at[i]))
        stores[-1].start()

    store(0, normed_v, normed_out)

    load_head.wait()
    lives = (HALF, voc - HALF)
    head_part = (head.at[0:HALF], head.at[HALF:voc])
    own_group = pl.ds(pl.multiple_of(vy * 16, 16), 16)
    lp[1, :, HALF - 128 :] = jnp.zeros((ROWS, 128), F32)

    def group(d):
        return pl.ds(pl.multiple_of(((vy + d) % NY) * 16, 16), 16)

    ways = ((0, 1, 2, 3, slice(0, HALF // 2)), (1, 7, 6, 5, slice(HALF // 2, HALF)))
    c1 = {}

    def first_sends(h):
        lp[h, :, : lives[h]] = lax.dot_general(
            normed, head_part[h][...], (((1,), (1,)), ((), ())), preferred_element_type=F32
        )
        for w, _, two, three, part4 in ways:
            i = 4 * h + 2 * w
            c1[h, w, 0] = start(
                copy(lp.at[h, group(4), part4], relay4.at[h, w], rl_s.at[i], rl_r.at[i], at_y(two))
            )
            c1[h, w, 1] = start(
                copy(lp.at[h, group(three)], relay.at[h, w], rl_s.at[i + 1], rl_r.at[i + 1], at_y(two))
            )

    first_sends(0)
    first_sends(1)
    cl = {}

    def pass_on(h):
        for w, one, two, _, part4 in ways:
            i = 4 * h + 2 * w
            c1[h, w, 0].wait_recv()
            lp[h, group(two), part4] += relay4[h, w]
            cl[h, w, 0] = start(
                copy(lp.at[h, group(two)], lrecv.at[h, 2 * w], lg_s.at[i], lg_r.at[i], at_y(two))
            )
            c1[h, w, 1].wait_recv()
            lp[h, group(one)] += relay[h, w]
            cl[h, w, 1] = start(
                copy(lp.at[h, group(one)], lrecv.at[h, 2 * w + 1], lg_s.at[i + 1], lg_r.at[i + 1], at_y(one))
            )

    is_target = []
    for h in range(2):
        entry = iota((ROWS, HALF), 1) + h * HALF
        is_target.append((entry + ctx * voc == tgt_c) & (entry < voc))

    def over_vocab(left):
        return sum(
            jnp.dot(left[h][:, : lives[h]], head_part[h][...], preferred_element_type=F32)
            for h in range(2)
        )

    def split(value, buf):
        for i in range(NX):
            for j in range(2):
                g = (i * 2 + j) * 16
                buf[j, i] = value[g : g + 16].astype(BF16)

    split(over_vocab([jnp.where(t, 1.0, 0.0).astype(BF16) for t in is_target]), tbuf)
    ct = start(copy(tbuf.at[1 - k], tcrecv, t_s.at[0], t_r.at[0], other))
    ct.wait_recv()
    txbuf[...] = (tbuf[k].astype(F32) + tcrecv[...].astype(F32)).astype(BF16)
    ct = {
        d: start(copy(txbuf.at[(x + d) % NX], txrecv.at[x], t_s.at[d], t_r.at[d], at_x(d)))
        for d in (2, 1, 3)
    }
    txrecv[x] = txbuf[x]
    pass_on(0)
    pass_on(1)
    for d in range(1, NX):
        ct[d].wait_recv()
    of_targets = jnp.sum(txrecv[...].astype(F32), axis=0)
    for j in range(NZ):
        tzbuf[j] = of_targets[:, j * 128 : (j + 1) * 128].astype(BF16)
    ct = {
        d: start(copy(tzbuf.at[(z + d) % NZ], tzrecv.at[z], t_s.at[8 + d], t_r.at[8 + d], at_z(d)))
        for d in FAR_FIRST
    }
    tzrecv[z] = tzbuf[z]

    to_lane = iota((16, ROWS), 1) == vy * 16 + iota((16, ROWS), 0)
    target16 = rows16(tgt_l, vy * 16).astype(jnp.int32) - ctx * voc
    stat_rows = []
    ce = {}
    for h in range(2):
        for w in range(2):
            cl[h, w, 0].wait_recv()
            cl[h, w, 1].wait_recv()
        logits = lp[h, own_group]
        for i in range(4):
            logits = logits + lrecv[h, i]
        lane = iota((16, HALF), 1)
        live = lane < lives[h]
        top = jnp.max(jnp.where(live, logits, -jnp.inf), axis=1, keepdims=True)
        shifted = logits - top
        exps = jnp.where(live, jnp.exp(shifted), 0.0)
        e_all[h, own_group] = exps.astype(BF16)
        stat = (
            top,
            jnp.sum(exps, axis=1, keepdims=True),
            jnp.sum(exps * shifted, axis=1, keepdims=True),
            jnp.sum(jnp.where(live & (lane + h * HALF == target16), logits, 0.0), axis=1, keepdims=True),
        )
        stat_rows += [jnp.sum(jnp.where(to_lane, v, 0.0), axis=0, keepdims=True) for v in stat]
        if h == 1:
            st_y[vy] = stack_rows(*stat_rows)
            cy = to_line(FAR_FIRST, vy, at_y, st_y, st_s, st_r, 0)
        for d in FAR_FIRST:
            ce[h, d] = start(
                copy(
                    e_all.at[h, own_group], e_all.at[h, own_group],
                    e_s.at[8 * h + d], e_r.at[8 * h + d], at_y(d),
                )
            )

    for d in range(1, NY):
        cy[d].wait_recv()
    block = jnp.sum(st_y[...], axis=0)
    tops = (block[0:1], block[4:5])
    here = combine([block[0:4], block[4:8]])
    st_c[k] = here
    cst = start(copy(st_c.at[k], st_c.at[k], st_s.at[20], st_r.at[20], other))

    u = None
    scales = columns(jnp.exp(tops[0] - here[0:1]), jnp.exp(tops[1] - here[0:1]))
    for h in range(2):
        for d in range(1, NY):
            ce[h, d].wait_recv()
        left = jnp.where(is_target[h], 0.0, scales[h] * e_all[h].astype(F32)).astype(BF16)
        part = jnp.dot(left[:, : lives[h]], head_part[h][...], preferred_element_type=F32)
        u = part if u is None else u + part
    split(u, ubuf)
    cu = start(copy(ubuf.at[1 - k], crecv, u_s.at[0], u_r.at[0], other))
    cst.wait_recv()
    by_core = combine([st_c[0], st_c[1]])
    st_x[x] = by_core
    cx = to_line((2, 1, 3), x, at_x, st_x, st_s, st_r, 16)
    own_l = jnp.exp(here[0:1] - by_core[0:1])
    other_l = jnp.exp(st_c[1 - k][0:1] - by_core[0:1])
    own_s = [rows16(own_l, (2 * i + k) * 16) for i in range(NX)]
    other_s = [rows16(other_l, (2 * i + k) * 16) for i in range(NX)]
    cu.wait_recv()
    for i in range(NX):
        xbuf[i] = (own_s[i] * ubuf[k, i].astype(F32) + other_s[i] * crecv[i].astype(F32)).astype(BF16)
    cu = {
        d: start(copy(xbuf.at[(x + d) % NX], xrecv.at[x], u_s.at[d], u_r.at[d], at_x(d)))
        for d in (2, 1, 3)
    }
    xrecv[x] = xbuf[x]
    for d in range(1, NX):
        cx[d].wait_recv()
    by_x = combine([st_x[i] for i in range(NX)])
    st_z[z] = by_x
    cz = to_line(FAR_FIRST, z, at_z, st_z, st_s, st_r, 8)
    first = (x * 2 + k) * 16
    r0 = pl.ds(pl.multiple_of(first, 16), 16)
    c0 = pl.ds(pl.multiple_of(z * 128, 128), 128)
    scales = [rows16(jnp.exp(st_x[i][0:1] - by_x[0:1]), first) for i in range(NX)]
    inv16 = rows16(inv_l, first)
    for d in range(1, NX):
        cu[d].wait_recv()
    part = scales[0] * xrecv[0].astype(F32)
    for i in range(1, NX):
        part = part + scales[i] * xrecv[i].astype(F32)
    for j in range(NZ):
        zbuf[j] = part[:, j * 128 : (j + 1) * 128].astype(BF16)
    cu = {
        d: start(copy(zbuf.at[(z + d) % NZ], zrecv.at[z], u_s.at[8 + d], u_r.at[8 + d], at_z(d)))
        for d in FAR_FIRST
    }
    zrecv[z] = zbuf[z]
    for d in range(1, NZ):
        cz[d].wait_recv()
    whole = combine([st_z[i] for i in range(NZ)])

    lanes1 = iota((1, ROWS), 1)
    den = jnp.where(lanes1 < SEQ_ROWS, den_ref[0], den_ref[1]).astype(F32)
    num = jnp.where(lanes1 < SEQ_ROWS, num_ref[0], num_ref[1]).astype(F32)
    factor = den / (num * (2.0 * MODEL))
    log_total = whole[0:1] + jnp.log(whole[1:2])
    target_l = whole[3:4]
    scaled = LOSS_SCALE * factor
    t_l = scaled * (jnp.exp(target_l - log_total) - 1.0)
    t16 = rows16(t_l, first)
    part = rows16(scaled * jnp.exp(by_x[0:1] - log_total), first) * part + t16 * of_targets
    gain_part = jnp.sum(part * rows[r0, :] * inv16, axis=0, keepdims=True)
    gg_p[x, z] = stack_rows(*(gain_part[:, j * 128 : (j + 1) * 128] for j in range(NZ)))
    cgg = to_plane(gg_p, ggp_s, ggp_r)

    loss = jnp.sum(factor * (log_total - target_l), axis=1, keepdims=True)
    small[8:16] = jnp.broadcast_to(loss, (8, ROWS))
    scales = [rows16(scaled * jnp.exp(st_z[i][0:1] - log_total), first) for i in range(NZ)]
    inner = scaled * (whole[2:3] / whole[1:2] + (whole[0:1] - target_l)) / (inv_l * float(MODEL))
    inner16 = rows16(inv_l * inv_l * inv_l * inner, first)
    for d in range(1, NZ):
        ct[d].wait_recv()
    of_targets = t16 * jnp.sum(tzrecv[...].astype(F32), axis=0)
    turned = inv16 * gain_ref[:, c0]
    taken = rows[r0, c0] * inner16
    for d in range(1, NZ):
        cu[d].wait_recv()
    dn = of_targets
    for i in range(NZ):
        dn = dn + scales[i] * zrecv[i].astype(F32)
    rg = turned * dn - taken
    xl = x % 2
    rgall[xl, k, z] = rg.astype(BF16)
    mine = rgall.at[xl, k, z]
    cg = {}
    for d in FAR_FIRST:
        cg[d] = start(copy(mine, mine, g_s.at[d], g_r.at[d], at_z(d)))
    for d in FAR_FIRST + (0,):
        cg[8 + d] = start(copy(mine, mine, g_s.at[8 + d], g_r.at[8 + d], at_pair(d)))
    t_c, *w_c = columns(t_l, *(scaled * jnp.exp(t - log_total) for t in tops))
    for h in range(2):
        dl = jnp.where(is_target[h], t_c, w_c[h] * e_all[h].astype(F32))
        dlt[h * HALF : (h + 1) * HALF] = dl.T.astype(BF16)
    store(1, dlt, dlt_out)
    for c in cgg:
        c.wait_recv()
    ggc[k] = jnp.sum(gg_p[...].reshape(NX * NZ, 8, 128), axis=0)
    cgc = start(copy(ggc.at[k], ggc.at[k], gg_s.at[0], gg_r.at[0], other))
    for c in cg.values():
        c.wait_recv()
    cgr = start(copy(rgall.at[:, k], rgall.at[:, k], g_s.at[16], g_r.at[16], other))
    cgc.wait_recv()
    small[0:8] = ggc[0] + ggc[1]
    store(2, small, small_out)
    for c in sent[:-1]:
        c.wait_send()
    cgr.wait_recv()
    store(3, rgall, rg_out)
    cgr.wait_send()
    for c in stores:
        c.wait()


def final_kernel(
    dlt_hbm, normed_hbm, rg_hbm, small_hbm, pos_hbm, gh_out, gx_out, gg_out, loss_out,
    dlt, normed, rg, small, pos_ref, gh, gx, sems,
):
    loads = []
    for i, (a, b) in enumerate(
        ((dlt_hbm, dlt), (normed_hbm, normed), (pos_hbm, pos_ref), (rg_hbm, rg), (small_hbm, small))
    ):
        loads.append(pltpu.make_async_copy(a, b, sems.at[i]))
        loads[-1].start()
    ctx = lax.axis_index("ctx")
    voc = gh.shape[0]
    for c in loads[:2]:
        c.wait()
    stores = []
    step = WIDTH // 4
    for i in range(4):
        c = slice(i * step, (i + 1) * step)
        gh[:, c] = jnp.dot(dlt[:voc], normed[:, c], preferred_element_type=F32).astype(BF16)
        stores.append(pltpu.make_async_copy(gh.at[:, c], gh_out.at[:, c], sems.at[8 + i]))
        stores[-1].start()
    for c in loads[2:]:
        c.wait()
    pos = jnp.where(ctx < 32, pos_ref[0:1], pos_ref[1:2])
    local = pos - (ctx % 32) * TOK
    spread = jnp.where(iota((TOK, SEQ_ROWS), 0) == local, 1.0, 0.0).astype(BF16)
    for j in range(NZ):
        piece = rg[:, :, j].reshape(SEQ_ROWS, 128)
        gx[:, j * 128 : (j + 1) * 128] = jnp.dot(spread, piece, preferred_element_type=F32).astype(BF16)
    stores.append(pltpu.make_async_copy(gx, gx_out, sems.at[5]))
    stores[-1].start()
    stores.append(pltpu.make_async_copy(small.at[0:8], gg_out, sems.at[6]))
    stores[-1].start()
    loss_out[0, 0] = small[8, 0]
    for c in stores:
        c.wait()


def on_device(hidden, norm_gain, head, masked_pos, masked_targets, t_num, t_den):
    voc = head.shape[0]
    sm = pl.BlockSpec(memory_space=pltpu.SMEM)
    hbm = pl.BlockSpec(memory_space=pltpu.HBM)
    V = pltpu.VMEM
    D = pltpu.SemaphoreType.DMA
    S = pltpu.SMEM
    I32 = jnp.int32
    shape = jax.ShapeDtypeStruct
    dlt, normed, rg, small = pl.pallas_call(
        main_kernel,
        name="main",
        out_shape=(
            shape((2 * HALF, ROWS), BF16),
            shape((ROWS, WIDTH), BF16),
            shape((2, 2, NZ, 16, 128), BF16),
            shape((16, 128), F32),
        ),
        in_specs=[hbm] * 7,
        out_specs=(hbm,) * 4,
        scratch_shapes=[
            V((TOK, WIDTH), BF16), V((1, WIDTH), F32), V((voc, WIDTH), BF16),
            V((2, SEQ_ROWS), I32), V((2, SEQ_ROWS), I32), S((2,), I32), S((2,), I32),
            V((NX, 2, NZ, 16, WIDTH // 2), BF16),
            V((ROWS, WIDTH), F32),
            V((2, ROWS, HALF), F32),
            V((2, 2, 16, HALF), F32),
            V((2, 2, 16, HALF // 2), F32),
            V((2, 4, 16, HALF), F32),
            V((2, ROWS, HALF), BF16),
            V((NY, 1, 128), F32), V((NX, NZ, 1, 128), F32), V((2, 1, 128), F32),
            V((NY, 8, 128), F32), V((NZ, 8, 128), F32), V((NX, 8, 128), F32), V((2, 8, 128), F32),
            V((2, NX, 16, WIDTH), BF16), V((NX, 16, WIDTH), BF16),
            V((NX, 16, WIDTH), BF16), V((NX, 16, WIDTH), BF16),
            V((NZ, 16, 128), BF16), V((NZ, 16, 128), BF16),
            V((2, NX, 16, WIDTH), BF16), V((NX, 16, WIDTH), BF16),
            V((NX, 16, WIDTH), BF16), V((NX, 16, WIDTH), BF16),
            V((NZ, 16, 128), BF16), V((NZ, 16, 128), BF16),
            V((2, 2, NZ, 16, 128), BF16),
            V((NX, NZ, 8, 128), F32), V((2, 8, 128), F32),
            V((2 * HALF, ROWS), BF16), V((ROWS, WIDTH), BF16), V((16, 128), F32),
            D((8,)),
            D((8,)), D((8,)), D((8, 4)), D((8, 4)), D((4,)), D((4,)),
            D((24,)), D((24,)), D((NX, NZ)), D((NX, NZ)), D((24,)), D((24,)), D((8,)), D((8,)), D((8,)), D((8,)), D((16,)), D((16,)),
            D((16,)), D((16,)), D((16,)), D((16,)), D((17,)), D((17,)), D((1,)), D((1,)), D((NX, NZ)), D((NX, NZ)),
        ],
        compiler_params=pltpu.CompilerParams(
            collective_id=0, has_side_effects=True, vmem_limit_bytes=60 << 20
        ),
    )(hidden, norm_gain.reshape(1, WIDTH), head, masked_pos, masked_targets, t_num, t_den)
    grad_head, grad_hidden, grad_gain, loss_value = pl.pallas_call(
        final_kernel,
        name="final",
        out_shape=(
            shape((voc, WIDTH), BF16),
            shape((TOK, WIDTH), BF16),
            shape((8, 128), F32),
            shape((1, 1), F32),
        ),
        in_specs=[hbm] * 5,
        out_specs=(hbm, hbm, hbm, sm),
        scratch_shapes=[
            V((2 * HALF, ROWS), BF16), V((ROWS, WIDTH), BF16), V((2, 2, NZ, 16, 128), BF16),
            V((16, 128), F32), V((2, SEQ_ROWS), I32),
            V((voc, WIDTH), BF16), V((TOK, WIDTH), BF16), D((12,)),
        ],
        compiler_params=pltpu.CompilerParams(vmem_limit_bytes=60 << 20),
    )(dlt, normed, rg, small, masked_pos)
    return (loss_value.reshape(()), grad_hidden, grad_head, grad_gain.reshape(WIDTH))


def solution(mesh):
    placed = (P("ctx", "vocab"), P("vocab"), P("ctx", "vocab"), P(), P(), P(), P())
    return jax.shard_map(
        on_device,
        mesh=mesh,
        in_specs=placed,
        out_specs=(P(), P("ctx", "vocab"), P("ctx", "vocab"), P("vocab")),
        check_vma=False,
    )
```

```python
import jax
import jax.numpy as jnp
from jax import lax
from jax.experimental import pallas as pl
from jax.experimental.pallas import tpu as pltpu
from jax.sharding import PartitionSpec as P

MESH = pl.DeviceIdType.MESH
F32 = jnp.float32
BF16 = jnp.bfloat16
EPSILON = 1e-05
LOSS_SCALE = 1024.0
NX, NZ, NY = 4, 8, 8
ROWS = 128
SEQ_ROWS = 64
TOK = 256
WIDTH = 1024
MODEL = 8192
HALF = 512
FAR_FIRST = (4, 3, 5, 2, 6, 1, 7)
NEAR_FIRST = (1, 7, 2, 6, 3, 5, 4)


def iota(shape, dim):
    return lax.broadcasted_iota(jnp.int32, shape, dim)


def column_of(lanes):
    n = lanes.shape[1]
    same = iota((n, n), 0) == iota((n, n), 1)
    return jnp.sum(jnp.where(same, lanes, 0.0), axis=1, keepdims=True)


def columns(*lanes):
    turned = stack_rows(*lanes).T
    return [turned[:, i : i + 1] for i in range(len(lanes))]


def rows16(lanes, start):
    same = iota((16, ROWS), 1) == start + iota((16, ROWS), 0)
    return jnp.sum(jnp.where(same, lanes, 0.0), axis=1, keepdims=True)


def lanes_of(column):
    n = column.shape[0]
    same = iota((n, n), 0) == iota((n, n), 1)
    return jnp.sum(jnp.where(same, column, 0.0), axis=0, keepdims=True)


def combine(tiles):
    top = tiles[0][0:1]
    for t in tiles[1:]:
        top = jnp.maximum(top, t[0:1])
    total = weighted = picked = None
    for t in tiles:
        shift = t[0:1] - top
        scale = jnp.exp(shift)
        a = scale * t[1:2]
        b = scale * (t[2:3] + shift * t[1:2])
        c = t[3:4]
        total = a if total is None else total + a
        weighted = b if weighted is None else weighted + b
        picked = c if picked is None else picked + c
    return stack_rows(top, total, weighted, picked)


def stack_rows(*rows):
    sub = iota((8, ROWS), 0)
    out = jnp.zeros((8, ROWS), F32)
    for i, r in enumerate(rows):
        out = jnp.where(sub == i, r, out)
    return out


def main_kernel(
    hidden_hbm, gain_hbm, head_hbm, pos_hbm, tgt_hbm, num_hbm, den_hbm,
    dlt_out, normed_out, rg_out, small_out,
    hidden, gain_ref, head, pos_ref, tgt_ref, num_ref, den_ref,
    slots, rows, lp, relay, relay4, lrecv, e_all,
    ss_y, ss_z, ss_x, ss_c, st_y, st_z, st_x, st_c,
    ubuf, crecv, xbuf, xrecv, zbuf, zrecv, tbuf, tcrecv, txbuf, txrecv, tzbuf, tzrecv, rgall, gg_p, ggc,
    dlt, normed_v, small, load_sem,
    row_z_s, row_z_r, row_x_s, row_x_r, row_c_s, row_c_r,
    ss_s, ss_r, st_s, st_r, rl_s, rl_r, lg_s, lg_r, e_s, e_r,
    u_s, u_r, t_s, t_r, g_s, g_r, gg_s, gg_r, ggp_s, ggp_r,
):
    ctx = lax.axis_index("ctx")
    vy = lax.axis_index("vocab")
    x = ctx // 16
    z = (ctx // 2) % NZ
    k = ctx % 2
    voc = head.shape[0]

    def at_x(d):
        return (((x + d) % NX) * 16 + z * 2 + k, vy)

    def at_z(d):
        return (x * 16 + ((z + d) % NZ) * 2 + k, vy)

    def at_y(d):
        return (ctx, (vy + d) % NY)

    pair_x = x + 1 - 2 * (x % 2)

    def at_pair(d):
        return (pair_x * 16 + ((z + d) % NZ) * 2 + k, vy)

    def at_xz(e, d):
        return (((x + e) % NX) * 16 + ((z + d) % NZ) * 2 + k, vy)

    plane = [(e, d) for d in FAR_FIRST + (0,) for e in (2, 1, 3, 0) if (e, d) != (0, 0)]
    other = (x * 16 + z * 2 + (1 - k), vy)

    barrier = pltpu.get_barrier_semaphore()
    peers = (
        [at_z(d) for d in FAR_FIRST]
        + [at_y(d) for d in FAR_FIRST]
        + [at_x(d) for d in (2, 1, 3)]
        + [other]
    )
    for p in peers:
        pl.semaphore_signal(barrier, inc=1, device_id=p, device_id_type=MESH)

    loads = []
    for i, (a, b) in enumerate(
        (
            (pos_hbm, pos_ref), (hidden_hbm, hidden), (tgt_hbm, tgt_ref), (gain_hbm, gain_ref),
            (num_hbm, num_ref), (den_hbm, den_ref), (head_hbm, head),
        )
    ):
        loads.append(pltpu.make_async_copy(a, b, load_sem.at[i]))
        loads[-1].start()
    load_head = loads[-1]

    def copy(src, dst, s, r, dev):
        return pltpu.make_async_remote_copy(
            src_ref=src, dst_ref=dst, send_sem=s, recv_sem=r, device_id=dev, device_id_type=MESH
        )

    sent = []

    def start(c):
        c.start()
        sent.append(c)
        return c

    def to_line(order, index, at, buf, ss_, rs_, base):
        return {d: start(copy(buf.at[index], buf.at[index], ss_.at[base + d], rs_.at[base + d], at(d))) for d in order}

    def to_plane(buf, ss_, rs_):
        mine = buf.at[x, z]
        return [start(copy(mine, mine, ss_.at[e, d], rs_.at[e, d], at_xz(e, d))) for e, d in plane]

    for c in loads[:-1]:
        c.wait()
    pos = pos_ref[...].astype(F32)
    tgt = tgt_ref[...].astype(F32)
    pos_c = jnp.concatenate([column_of(pos[0:1]), column_of(pos[1:2]) + float(MODEL)], axis=0)
    tgt_c = jnp.concatenate([column_of(tgt[0:1]), column_of(tgt[1:2])], axis=0)
    tgt_l = lanes_of(tgt_c)
    tgt_c = tgt_c.astype(jnp.int32)
    pos_i = pos_c.astype(jnp.int32)
    owner_c = pos_i >> 8
    owner_l = lanes_of(owner_c.astype(F32))
    chosen = jnp.where(pos_i == ctx * TOK + iota((ROWS, TOK), 1), 1.0, 0.0)
    pick = jnp.sum(chosen.reshape(ROWS // 8, 8, TOK), axis=0).astype(BF16)
    own = jnp.dot(pick, hidden[...], preferred_element_type=F32)
    half = WIDTH // 2
    slots[x, k, z] = jnp.concatenate([own[:, :half], own[:, half:]], axis=0).astype(BF16)
    squares = jnp.sum(own * own, axis=1, keepdims=True)
    lane8 = iota((8, ROWS), 1)
    mine = (lane8 % 8 == iota((8, ROWS), 0)) & (owner_l == ctx.astype(F32))
    ss = jnp.sum(jnp.where(mine, squares, 0.0), axis=0, keepdims=True)
    ss_y[vy] = ss

    pl.semaphore_wait(barrier, len(peers))

    cz = to_line(FAR_FIRST, (x, k, z), at_z, slots, row_z_s, row_z_r, 0)
    cy = to_line(FAR_FIRST, vy, at_y, ss_y, ss_s, ss_r, 0)
    cx = {}

    def forward_x(d):
        zz = (z - d + NZ) % NZ
        for e in (2, 1, 3):
            cx[d, e] = start(
                copy(slots.at[x, k, zz], slots.at[x, k, zz], row_x_s.at[d, e], row_x_r.at[d, e], at_x(e))
            )

    forward_x(0)
    for d in NEAR_FIRST[:4]:
        cz[d].wait_recv()
        forward_x(d)
    for d in range(1, NY):
        cy[d].wait_recv()
    ss_z[z] = jnp.sum(ss_y[...], axis=0)
    cssz = to_line(FAR_FIRST, z, at_z, ss_z, ss_s, ss_r, 8)
    for d in NEAR_FIRST[4:]:
        cz[d].wait_recv()
        forward_x(d)
    cc = {}

    def forward_core(e):
        xx = (x - e + NX) % NX
        cc[e] = start(copy(slots.at[xx, k], slots.at[xx, k], row_c_s.at[e], row_c_r.at[e], other))

    forward_core(0)
    for d in range(1, NZ):
        cssz[d].wait_recv()
    ss_x[x] = jnp.sum(ss_z[...], axis=0)
    cssx = to_line((2, 1, 3), x, at_x, ss_x, ss_s, ss_r, 16)
    for e in (1, 3, 2):
        for d in range(NZ):
            cx[d, e].wait_recv()
        forward_core(e)
    for e in range(1, NX):
        cssx[e].wait_recv()
    ss_c[k] = jnp.sum(ss_x[...], axis=0)
    css = start(copy(ss_c.at[k], ss_c.at[k], ss_s.at[20], ss_r.at[20], other))
    for e in range(NX):
        cc[e].wait_recv()

    seq_block = owner_c - jnp.where(iota((ROWS, 1), 0) >= SEQ_ROWS, 32, 0)
    place = ((seq_block >> 4) * 16 + (seq_block & 1) * 8 + ((seq_block >> 1) & 7)) * 16 + (
        iota((ROWS, 1), 0) & 7
    )
    lane512 = iota((SEQ_ROWS, 512), 1)
    for s in range(2):
        here = place[s * SEQ_ROWS : (s + 1) * SEQ_ROWS]
        piece = slots[2 * s : 2 * s + 2].reshape(512, half)
        for h in range(2):
            spread = jnp.where(lane512 == here + 8 * h, 1.0, 0.0).astype(BF16)
            rows[s * SEQ_ROWS : (s + 1) * SEQ_ROWS, h * half : (h + 1) * half] = jnp.dot(
                spread, piece, preferred_element_type=F32
            )
    css.wait_recv()
    squares_l = ss_c[0] + ss_c[1]
    inv_l = lax.rsqrt(squares_l / float(MODEL) + EPSILON)
    [inv_c] = columns(inv_l)
    normed = (rows[...] * inv_c * gain_ref[...]).astype(BF16)
    normed_v[...] = normed
    stores = []

    def store(i, a, b):
        stores.append(pltpu.make_async_copy(a, b, load_sem.at[i]))
        stores[-1].start()

    store(0, normed_v, normed_out)

    load_head.wait()
    lives = (HALF, voc - HALF)
    head_part = (head.at[0:HALF], head.at[HALF:voc])
    own_group = pl.ds(pl.multiple_of(vy * 16, 16), 16)
    lp[1, :, HALF - 128 :] = jnp.zeros((ROWS, 128), F32)

    def group(d):
        return pl.ds(pl.multiple_of(((vy + d) % NY) * 16, 16), 16)

    ways = ((0, 1, 2, 3, slice(0, HALF // 2)), (1, 7, 6, 5, slice(HALF // 2, HALF)))
    c1 = {}

    def first_sends(h):
        lp[h, :, : lives[h]] = lax.dot_general(
            normed, head_part[h][...], (((1,), (1,)), ((), ())), preferred_element_type=F32
        )
        for w, _, two, three, part4 in ways:
            i = 4 * h + 2 * w
            c1[h, w, 0] = start(
                copy(lp.at[h, group(4), part4], relay4.at[h, w], rl_s.at[i], rl_r.at[i], at_y(two))
            )
            c1[h, w, 1] = start(
                copy(lp.at[h, group(three)], relay.at[h, w], rl_s.at[i + 1], rl_r.at[i + 1], at_y(two))
            )

    first_sends(0)
    first_sends(1)
    cl = {}

    def pass_on(h):
        for w, one, two, _, part4 in ways:
            i = 4 * h + 2 * w
            c1[h, w, 0].wait_recv()
            lp[h, group(two), part4] += relay4[h, w]
            cl[h, w, 0] = start(
                copy(lp.at[h, group(two)], lrecv.at[h, 2 * w], lg_s.at[i], lg_r.at[i], at_y(two))
            )
            c1[h, w, 1].wait_recv()
            lp[h, group(one)] += relay[h, w]
            cl[h, w, 1] = start(
                copy(lp.at[h, group(one)], lrecv.at[h, 2 * w + 1], lg_s.at[i + 1], lg_r.at[i + 1], at_y(one))
            )

    is_target = []
    for h in range(2):
        entry = iota((ROWS, HALF), 1) + h * HALF
        is_target.append((entry + ctx * voc == tgt_c) & (entry < voc))

    def over_vocab(left):
        return sum(
            jnp.dot(left[h][:, : lives[h]], head_part[h][...], preferred_element_type=F32)
            for h in range(2)
        )

    def split(value, buf):
        for i in range(NX):
            for j in range(2):
                g = (i * 2 + j) * 16
                buf[j, i] = value[g : g + 16].astype(BF16)

    split(over_vocab([jnp.where(t, 1.0, 0.0).astype(BF16) for t in is_target]), tbuf)
    ct = start(copy(tbuf.at[1 - k], tcrecv, t_s.at[0], t_r.at[0], other))
    ct.wait_recv()
    txbuf[...] = (tbuf[k].astype(F32) + tcrecv[...].astype(F32)).astype(BF16)
    ct = {
        d: start(copy(txbuf.at[(x + d) % NX], txrecv.at[x], t_s.at[d], t_r.at[d], at_x(d)))
        for d in (2, 1, 3)
    }
    txrecv[x] = txbuf[x]
    pass_on(0)
    pass_on(1)
    for d in range(1, NX):
        ct[d].wait_recv()
    of_targets = jnp.sum(txrecv[...].astype(F32), axis=0)
    for j in range(NZ):
        tzbuf[j] = of_targets[:, j * 128 : (j + 1) * 128].astype(BF16)
    ct = {
        d: start(copy(tzbuf.at[(z + d) % NZ], tzrecv.at[z], t_s.at[8 + d], t_r.at[8 + d], at_z(d)))
        for d in FAR_FIRST
    }
    tzrecv[z] = tzbuf[z]

    to_lane = iota((16, ROWS), 1) == vy * 16 + iota((16, ROWS), 0)
    target16 = rows16(tgt_l, vy * 16).astype(jnp.int32) - ctx * voc
    stat_rows = []
    ce = {}
    for h in range(2):
        for w in range(2):
            cl[h, w, 0].wait_recv()
            cl[h, w, 1].wait_recv()
        logits = lp[h, own_group]
        for i in range(4):
            logits = logits + lrecv[h, i]
        lane = iota((16, HALF), 1)
        live = lane < lives[h]
        top = jnp.max(jnp.where(live, logits, -jnp.inf), axis=1, keepdims=True)
        shifted = logits - top
        exps = jnp.where(live, jnp.exp(shifted), 0.0)
        e_all[h, own_group] = exps.astype(BF16)
        stat = (
            top,
            jnp.sum(exps, axis=1, keepdims=True),
            jnp.sum(exps * shifted, axis=1, keepdims=True),
            jnp.sum(jnp.where(live & (lane + h * HALF == target16), logits, 0.0), axis=1, keepdims=True),
        )
        stat_rows += [jnp.sum(jnp.where(to_lane, v, 0.0), axis=0, keepdims=True) for v in stat]
        if h == 1:
            st_y[vy] = stack_rows(*stat_rows)
            cy = to_line(FAR_FIRST, vy, at_y, st_y, st_s, st_r, 0)
        for d in FAR_FIRST:
            ce[h, d] = start(
                copy(
                    e_all.at[h, own_group], e_all.at[h, own_group],
                    e_s.at[8 * h + d], e_r.at[8 * h + d], at_y(d),
                )
            )

    for d in range(1, NY):
        cy[d].wait_recv()
    block = jnp.sum(st_y[...], axis=0)
    tops = (block[0:1], block[4:5])
    here = combine([block[0:4], block[4:8]])
    st_c[k] = here
    cst = start(copy(st_c.at[k], st_c.at[k], st_s.at[20], st_r.at[20], other))

    u = None
    scales = columns(jnp.exp(tops[0] - here[0:1]), jnp.exp(tops[1] - here[0:1]))
    for h in range(2):
        for d in range(1, NY):
            ce[h, d].wait_recv()
        left = jnp.where(is_target[h], 0.0, scales[h] * e_all[h].astype(F32)).astype(BF16)
        part = jnp.dot(left[:, : lives[h]], head_part[h][...], preferred_element_type=F32)
        u = part if u is None else u + part
    split(u, ubuf)
    cu = start(copy(ubuf.at[1 - k], crecv, u_s.at[0], u_r.at[0], other))
    cst.wait_recv()
    by_core = combine([st_c[0], st_c[1]])
    st_x[x] = by_core
    cx = to_line((2, 1, 3), x, at_x, st_x, st_s, st_r, 16)
    own_l = jnp.exp(here[0:1] - by_core[0:1])
    other_l = jnp.exp(st_c[1 - k][0:1] - by_core[0:1])
    own_s = [rows16(own_l, (2 * i + k) * 16) for i in range(NX)]
    other_s = [rows16(other_l, (2 * i + k) * 16) for i in range(NX)]
    cu.wait_recv()
    for i in range(NX):
        xbuf[i] = (own_s[i] * ubuf[k, i].astype(F32) + other_s[i] * crecv[i].astype(F32)).astype(BF16)
    cu = {
        d: start(copy(xbuf.at[(x + d) % NX], xrecv.at[x], u_s.at[d], u_r.at[d], at_x(d)))
        for d in (2, 1, 3)
    }
    xrecv[x] = xbuf[x]
    for d in range(1, NX):
        cx[d].wait_recv()
    by_x = combine([st_x[i] for i in range(NX)])
    st_z[z] = by_x
    cz = to_line(FAR_FIRST, z, at_z, st_z, st_s, st_r, 8)
    first = (x * 2 + k) * 16
    r0 = pl.ds(pl.multiple_of(first, 16), 16)
    c0 = pl.ds(pl.multiple_of(z * 128, 128), 128)
    scales = [rows16(jnp.exp(st_x[i][0:1] - by_x[0:1]), first) for i in range(NX)]
    inv16 = rows16(inv_l, first)
    for d in range(1, NX):
        cu[d].wait_recv()
    part = scales[0] * xrecv[0].astype(F32)
    for i in range(1, NX):
        part = part + scales[i] * xrecv[i].astype(F32)
    for j in range(NZ):
        zbuf[j] = part[:, j * 128 : (j + 1) * 128].astype(BF16)
    cu = {
        d: start(copy(zbuf.at[(z + d) % NZ], zrecv.at[z], u_s.at[8 + d], u_r.at[8 + d], at_z(d)))
        for d in FAR_FIRST
    }
    zrecv[z] = zbuf[z]
    for d in range(1, NZ):
        cz[d].wait_recv()
    whole = combine([st_z[i] for i in range(NZ)])

    lanes1 = iota((1, ROWS), 1)
    den = jnp.where(lanes1 < SEQ_ROWS, den_ref[0], den_ref[1]).astype(F32)
    num = jnp.where(lanes1 < SEQ_ROWS, num_ref[0], num_ref[1]).astype(F32)
    factor = den / (num * (2.0 * MODEL))
    log_total = whole[0:1] + jnp.log(whole[1:2])
    target_l = whole[3:4]
    scaled = LOSS_SCALE * factor
    t_l = scaled * (jnp.exp(target_l - log_total) - 1.0)
    t16 = rows16(t_l, first)
    part = rows16(scaled * jnp.exp(by_x[0:1] - log_total), first) * part + t16 * of_targets
    gain_part = jnp.sum(part * rows[r0, :] * inv16, axis=0, keepdims=True)
    gg_p[x, z] = stack_rows(*(gain_part[:, j * 128 : (j + 1) * 128] for j in range(NZ)))
    cgg = to_plane(gg_p, ggp_s, ggp_r)

    loss = jnp.sum(factor * (log_total - target_l), axis=1, keepdims=True)
    small[8:16] = jnp.broadcast_to(loss, (8, ROWS))
    scales = [rows16(scaled * jnp.exp(st_z[i][0:1] - log_total), first) for i in range(NZ)]
    inner = scaled * (whole[2:3] / whole[1:2] + (whole[0:1] - target_l)) / (inv_l * float(MODEL))
    inner16 = rows16(inv_l * inv_l * inv_l * inner, first)
    for d in range(1, NZ):
        ct[d].wait_recv()
    of_targets = t16 * jnp.sum(tzrecv[...].astype(F32), axis=0)
    turned = inv16 * gain_ref[:, c0]
    taken = rows[r0, c0] * inner16
    for d in range(1, NZ):
        cu[d].wait_recv()
    dn = of_targets
    for i in range(NZ):
        dn = dn + scales[i] * zrecv[i].astype(F32)
    rg = turned * dn - taken
    xl = x % 2
    rgall[xl, k, z] = rg.astype(BF16)
    mine = rgall.at[xl, k, z]
    cg = {}
    for d in FAR_FIRST:
        cg[d] = start(copy(mine, mine, g_s.at[d], g_r.at[d], at_z(d)))
    for d in FAR_FIRST + (0,):
        cg[8 + d] = start(copy(mine, mine, g_s.at[8 + d], g_r.at[8 + d], at_pair(d)))
    t_c, *w_c = columns(t_l, *(scaled * jnp.exp(t - log_total) for t in tops))
    for h in range(2):
        dl = jnp.where(is_target[h], t_c, w_c[h] * e_all[h].astype(F32))
        dlt[h * HALF : (h + 1) * HALF] = dl.T.astype(BF16)
    store(1, dlt, dlt_out)
    for c in cgg:
        c.wait_recv()
    ggc[k] = jnp.sum(gg_p[...].reshape(NX * NZ, 8, 128), axis=0)
    cgc = start(copy(ggc.at[k], ggc.at[k], gg_s.at[0], gg_r.at[0], other))
    for c in cg.values():
        c.wait_recv()
    cgr = start(copy(rgall.at[:, k], rgall.at[:, k], g_s.at[16], g_r.at[16], other))
    cgc.wait_recv()
    small[0:8] = ggc[0] + ggc[1]
    store(2, small, small_out)
    for c in sent[:-1]:
        c.wait_send()
    cgr.wait_recv()
    store(3, rgall, rg_out)
    cgr.wait_send()
    for c in stores:
        c.wait()


def final_kernel(
    dlt_hbm, normed_hbm, rg_hbm, small_hbm, pos_hbm, gh_out, gx_out, gg_out, loss_out,
    dlt, normed, rg, small, pos_ref, gh, gx, sems,
):
    loads = []
    for i, (a, b) in enumerate(
        ((dlt_hbm, dlt), (normed_hbm, normed), (pos_hbm, pos_ref), (rg_hbm, rg), (small_hbm, small))
    ):
        loads.append(pltpu.make_async_copy(a, b, sems.at[i]))
        loads[-1].start()
    ctx = lax.axis_index("ctx")
    voc = gh.shape[0]
    for c in loads[:2]:
        c.wait()
    stores = []
    step = WIDTH // 4
    for i in range(4):
        c = slice(i * step, (i + 1) * step)
        gh[:, c] = jnp.dot(dlt[:voc], normed[:, c], preferred_element_type=F32).astype(BF16)
        stores.append(pltpu.make_async_copy(gh.at[:, c], gh_out.at[:, c], sems.at[8 + i]))
        stores[-1].start()
    for c in loads[2:]:
        c.wait()
    pos = jnp.where(ctx < 32, pos_ref[0:1], pos_ref[1:2])
    local = pos - (ctx % 32) * TOK
    spread = jnp.where(iota((TOK, SEQ_ROWS), 0) == local, 1.0, 0.0).astype(BF16)
    for j in range(NZ):
        piece = rg[:, :, j].reshape(SEQ_ROWS, 128)
        gx[:, j * 128 : (j + 1) * 128] = jnp.dot(spread, piece, preferred_element_type=F32).astype(BF16)
    stores.append(pltpu.make_async_copy(gx, gx_out, sems.at[5]))
    stores[-1].start()
    stores.append(pltpu.make_async_copy(small.at[0:8], gg_out, sems.at[6]))
    stores[-1].start()
    loss_out[0, 0] = small[8, 0]
    for c in stores:
        c.wait()


def on_device(hidden, norm_gain, head, masked_pos, masked_targets, t_num, t_den):
    voc = head.shape[0]
    sm = pl.BlockSpec(memory_space=pltpu.SMEM)
    hbm = pl.BlockSpec(memory_space=pltpu.HBM)
    V = pltpu.VMEM
    D = pltpu.SemaphoreType.DMA
    S = pltpu.SMEM
    I32 = jnp.int32
    shape = jax.ShapeDtypeStruct
    dlt, normed, rg, small = pl.pallas_call(
        main_kernel,
        name="main",
        out_shape=(
            shape((2 * HALF, ROWS), BF16),
            shape((ROWS, WIDTH), BF16),
            shape((2, 2, NZ, 16, 128), BF16),
            shape((16, 128), F32),
        ),
        in_specs=[hbm] * 7,
        out_specs=(hbm,) * 4,
        scratch_shapes=[
            V((TOK, WIDTH), BF16), V((1, WIDTH), F32), V((voc, WIDTH), BF16),
            V((2, SEQ_ROWS), I32), V((2, SEQ_ROWS), I32), S((2,), I32), S((2,), I32),
            V((NX, 2, NZ, 16, WIDTH // 2), BF16),
            V((ROWS, WIDTH), F32),
            V((2, ROWS, HALF), F32),
            V((2, 2, 16, HALF), F32),
            V((2, 2, 16, HALF // 2), F32),
            V((2, 4, 16, HALF), F32),
            V((2, ROWS, HALF), BF16),
            V((NY, 1, 128), F32), V((NZ, 1, 128), F32), V((NX, 1, 128), F32), V((2, 1, 128), F32),
            V((NY, 8, 128), F32), V((NZ, 8, 128), F32), V((NX, 8, 128), F32), V((2, 8, 128), F32),
            V((2, NX, 16, WIDTH), BF16), V((NX, 16, WIDTH), BF16),
            V((NX, 16, WIDTH), BF16), V((NX, 16, WIDTH), BF16),
            V((NZ, 16, 128), BF16), V((NZ, 16, 128), BF16),
            V((2, NX, 16, WIDTH), BF16), V((NX, 16, WIDTH), BF16),
            V((NX, 16, WIDTH), BF16), V((NX, 16, WIDTH), BF16),
            V((NZ, 16, 128), BF16), V((NZ, 16, 128), BF16),
            V((2, 2, NZ, 16, 128), BF16),
            V((NX, NZ, 8, 128), F32), V((2, 8, 128), F32),
            V((2 * HALF, ROWS), BF16), V((ROWS, WIDTH), BF16), V((16, 128), F32),
            D((8,)),
            D((8,)), D((8,)), D((8, 4)), D((8, 4)), D((4,)), D((4,)),
            D((24,)), D((24,)), D((24,)), D((24,)), D((8,)), D((8,)), D((8,)), D((8,)), D((16,)), D((16,)),
            D((16,)), D((16,)), D((16,)), D((16,)), D((17,)), D((17,)), D((1,)), D((1,)), D((NX, NZ)), D((NX, NZ)),
        ],
        compiler_params=pltpu.CompilerParams(
            collective_id=0, has_side_effects=True, vmem_limit_bytes=60 << 20
        ),
    )(hidden, norm_gain.reshape(1, WIDTH), head, masked_pos, masked_targets, t_num, t_den)
    grad_head, grad_hidden, grad_gain, loss_value = pl.pallas_call(
        final_kernel,
        name="final",
        out_shape=(
            shape((voc, WIDTH), BF16),
            shape((TOK, WIDTH), BF16),
            shape((8, 128), F32),
            shape((1, 1), F32),
        ),
        in_specs=[hbm] * 5,
        out_specs=(hbm, hbm, hbm, sm),
        scratch_shapes=[
            V((2 * HALF, ROWS), BF16), V((ROWS, WIDTH), BF16), V((2, 2, NZ, 16, 128), BF16),
            V((16, 128), F32), V((2, SEQ_ROWS), I32),
            V((voc, WIDTH), BF16), V((TOK, WIDTH), BF16), D((12,)),
        ],
        compiler_params=pltpu.CompilerParams(vmem_limit_bytes=60 << 20),
    )(dlt, normed, rg, small, masked_pos)
    return (loss_value.reshape(()), grad_hidden, grad_head, grad_gain.reshape(WIDTH))


def solution(mesh):
    placed = (P("ctx", "vocab"), P("vocab"), P("ctx", "vocab"), P(), P(), P(), P())
    return jax.shard_map(
        on_device,
        mesh=mesh,
        in_specs=placed,
        out_specs=(P(), P("ctx", "vocab"), P("ctx", "vocab"), P("vocab")),
        check_vma=False,
    )
```

```python
import jax
import jax.numpy as jnp
from jax import lax
from jax.experimental import pallas as pl
from jax.experimental.pallas import tpu as pltpu
from jax.sharding import PartitionSpec as P

MESH = pl.DeviceIdType.MESH
F32 = jnp.float32
BF16 = jnp.bfloat16
EPSILON = 1e-05
LOSS_SCALE = 1024.0
NX, NZ, NY = 4, 8, 8
ROWS = 128
SEQ_ROWS = 64
TOK = 256
WIDTH = 1024
MODEL = 8192
PARTS = 2
PART = 1024 // PARTS
FAR_FIRST = (4, 3, 5, 2, 6, 1, 7)
NEAR_FIRST = (1, 7, 2, 6, 3, 5, 4)


def iota(shape, dim):
    return lax.broadcasted_iota(jnp.int32, shape, dim)


def column_of(lanes):
    n = lanes.shape[1]
    same = iota((n, n), 0) == iota((n, n), 1)
    return jnp.sum(jnp.where(same, lanes, 0.0), axis=1, keepdims=True)


def columns(*lanes):
    turned = stack_rows(*lanes).T
    return [turned[:, i : i + 1] for i in range(len(lanes))]


def rows16(lanes, start):
    same = iota((16, ROWS), 1) == start + iota((16, ROWS), 0)
    return jnp.sum(jnp.where(same, lanes, 0.0), axis=1, keepdims=True)


def lanes_of(column):
    n = column.shape[0]
    same = iota((n, n), 0) == iota((n, n), 1)
    return jnp.sum(jnp.where(same, column, 0.0), axis=0, keepdims=True)


def combine(tiles):
    top = tiles[0][0:1]
    for t in tiles[1:]:
        top = jnp.maximum(top, t[0:1])
    total = weighted = picked = None
    for t in tiles:
        shift = t[0:1] - top
        scale = jnp.exp(shift)
        a = scale * t[1:2]
        b = scale * (t[2:3] + shift * t[1:2])
        c = t[3:4]
        total = a if total is None else total + a
        weighted = b if weighted is None else weighted + b
        picked = c if picked is None else picked + c
    return stack_rows(top, total, weighted, picked)


def stack_rows(*rows):
    sub = iota((8, ROWS), 0)
    out = jnp.zeros((8, ROWS), F32)
    for i, r in enumerate(rows):
        out = jnp.where(sub == i, r, out)
    return out


def main_kernel(
    hidden_hbm, gain_hbm, head_hbm, pos_hbm, tgt_hbm, num_hbm, den_hbm,
    dlt_out, normed_out, rg_out, small_out,
    hidden, gain_ref, head, pos_ref, tgt_ref, num_ref, den_ref,
    slots, rows, lp, relay, relay4, lrecv, e_all,
    ss_y, ss_z, ss_x, ss_c, st_y, st_z, st_x, st_c,
    ubuf, crecv, xbuf, xrecv, zbuf, zrecv, tbuf, tcrecv, txbuf, txrecv, tzbuf, tzrecv, rgall, gg_p, ggc,
    dlt, normed_v, small, load_sem,
    row_z_s, row_z_r, row_x_s, row_x_r, row_c_s, row_c_r,
    ss_s, ss_r, st_s, st_r, rl_s, rl_r, lg_s, lg_r, e_s, e_r,
    u_s, u_r, t_s, t_r, g_s, g_r, gg_s, gg_r, ggp_s, ggp_r,
):
    ctx = lax.axis_index("ctx")
    vy = lax.axis_index("vocab")
    x = lax.div(ctx, 16)
    z = lax.rem(lax.div(ctx, 2), NZ)
    k = lax.rem(ctx, 2)
    voc = head.shape[0]

    xs = [x] + [lax.rem(x + d, NX) for d in range(1, NX)]
    zs = [z] + [lax.rem(z + d, NZ) for d in range(1, NZ)]
    ys = [vy] + [lax.rem(vy + d, NY) for d in range(1, NY)]
    pair_x = x + 1 - 2 * lax.rem(x, 2)
    x16 = [i * 16 for i in xs]
    z2k = [i * 2 + k for i in zs]

    def at_x(d):
        return (x16[d] + z2k[0], vy)

    def at_z(d):
        return (x16[0] + z2k[d], vy)

    def at_y(d):
        return (ctx, ys[d])

    def at_pair(d):
        return (pair_x * 16 + z2k[d], vy)

    def at_xz(e, d):
        return (x16[e] + z2k[d], vy)

    plane = [(e, d) for d in FAR_FIRST + (0,) for e in (2, 1, 3, 0) if (e, d) != (0, 0)]
    other = (x * 16 + z * 2 + (1 - k), vy)

    barrier = pltpu.get_barrier_semaphore()
    peers = (
        [at_z(d) for d in FAR_FIRST]
        + [at_y(d) for d in FAR_FIRST]
        + [at_x(d) for d in (2, 1, 3)]
        + [other]
    )
    for p in peers:
        pl.semaphore_signal(barrier, inc=1, device_id=p, device_id_type=MESH)

    loads = []
    for i, (a, b) in enumerate(
        (
            (pos_hbm, pos_ref), (hidden_hbm, hidden), (tgt_hbm, tgt_ref), (gain_hbm, gain_ref),
            (num_hbm, num_ref), (den_hbm, den_ref), (head_hbm, head),
        )
    ):
        loads.append(pltpu.make_async_copy(a, b, load_sem.at[i]))
        loads[-1].start()
    load_head = loads[-1]

    def copy(src, dst, s, r, dev):
        return pltpu.make_async_remote_copy(
            src_ref=src, dst_ref=dst, send_sem=s, recv_sem=r, device_id=dev, device_id_type=MESH
        )

    sent = []

    def start(c):
        c.start()
        sent.append(c)
        return c

    def to_line(order, index, at, buf, ss_, rs_, base):
        return {d: start(copy(buf.at[index], buf.at[index], ss_.at[base + d], rs_.at[base + d], at(d))) for d in order}

    def to_plane(buf, ss_, rs_):
        mine = buf.at[x, z]
        return [start(copy(mine, mine, ss_.at[e, d], rs_.at[e, d], at_xz(e, d))) for e, d in plane]

    for c in loads[:-1]:
        c.wait()
    pos = pos_ref[...].astype(F32)
    tgt = tgt_ref[...].astype(F32)
    pos_c = jnp.concatenate([column_of(pos[0:1]), column_of(pos[1:2]) + float(MODEL)], axis=0)
    tgt_c = jnp.concatenate([column_of(tgt[0:1]), column_of(tgt[1:2])], axis=0)
    tgt_l = lanes_of(tgt_c)
    tgt_c = tgt_c.astype(jnp.int32)
    pos_i = pos_c.astype(jnp.int32)
    owner_c = pos_i >> 8
    owner_l = lanes_of(owner_c.astype(F32))
    chosen = jnp.where(pos_i == ctx * TOK + iota((ROWS, TOK), 1), 1.0, 0.0)
    pick = jnp.sum(chosen.reshape(ROWS // 8, 8, TOK), axis=0).astype(BF16)
    own = jnp.dot(pick, hidden[...], preferred_element_type=F32)
    half = WIDTH // 2
    slots[x, k, z] = jnp.concatenate([own[:, :half], own[:, half:]], axis=0).astype(BF16)
    squares = jnp.sum(own * own, axis=1, keepdims=True)
    lane8 = iota((8, ROWS), 1)
    mine = (lane8 % 8 == iota((8, ROWS), 0)) & (owner_l == ctx.astype(F32))
    ss = jnp.sum(jnp.where(mine, squares, 0.0), axis=0, keepdims=True)
    ss_y[vy] = ss

    pl.semaphore_wait(barrier, len(peers))

    cz = to_line(FAR_FIRST, (x, k, z), at_z, slots, row_z_s, row_z_r, 0)
    cy = to_line(FAR_FIRST, vy, at_y, ss_y, ss_s, ss_r, 0)
    cx = {}

    def forward_x(d):
        zz = zs[(NZ - d) % NZ]
        for e in (2, 1, 3):
            cx[d, e] = start(
                copy(slots.at[x, k, zz], slots.at[x, k, zz], row_x_s.at[d, e], row_x_r.at[d, e], at_x(e))
            )

    forward_x(0)
    for d in NEAR_FIRST[:4]:
        cz[d].wait_recv()
        forward_x(d)
    for d in range(1, NY):
        cy[d].wait_recv()
    ss_z[z] = jnp.sum(ss_y[...], axis=0)
    cssz = to_line(FAR_FIRST, z, at_z, ss_z, ss_s, ss_r, 8)
    for d in NEAR_FIRST[4:]:
        cz[d].wait_recv()
        forward_x(d)
    cc = {}

    def forward_core(e):
        xx = xs[(NX - e) % NX]
        cc[e] = start(copy(slots.at[xx, k], slots.at[xx, k], row_c_s.at[e], row_c_r.at[e], other))

    forward_core(0)
    for d in range(1, NZ):
        cssz[d].wait_recv()
    ss_x[x] = jnp.sum(ss_z[...], axis=0)
    cssx = to_line((2, 1, 3), x, at_x, ss_x, ss_s, ss_r, 16)
    for e in (1, 3, 2):
        for d in range(NZ):
            cx[d, e].wait_recv()
        forward_core(e)
    for e in range(1, NX):
        cssx[e].wait_recv()
    ss_c[k] = jnp.sum(ss_x[...], axis=0)
    css = start(copy(ss_c.at[k], ss_c.at[k], ss_s.at[20], ss_r.at[20], other))
    for e in range(NX):
        cc[e].wait_recv()

    seq_block = owner_c - jnp.where(iota((ROWS, 1), 0) >= SEQ_ROWS, 32, 0)
    place = ((seq_block >> 4) * 16 + (seq_block & 1) * 8 + ((seq_block >> 1) & 7)) * 16 + (
        iota((ROWS, 1), 0) & 7
    )
    lane512 = iota((SEQ_ROWS, 512), 1)
    for s in range(2):
        here = place[s * SEQ_ROWS : (s + 1) * SEQ_ROWS]
        piece = slots[2 * s : 2 * s + 2].reshape(512, half)
        for h in range(2):
            spread = jnp.where(lane512 == here + 8 * h, 1.0, 0.0).astype(BF16)
            rows[s * SEQ_ROWS : (s + 1) * SEQ_ROWS, h * half : (h + 1) * half] = jnp.dot(
                spread, piece, preferred_element_type=F32
            )
    css.wait_recv()
    squares_l = ss_c[0] + ss_c[1]
    inv_l = lax.rsqrt(squares_l / float(MODEL) + EPSILON)
    [inv_c] = columns(inv_l)
    normed = (rows[...] * inv_c * gain_ref[...]).astype(BF16)
    normed_v[...] = normed
    stores = []

    def store(i, a, b):
        stores.append(pltpu.make_async_copy(a, b, load_sem.at[i]))
        stores[-1].start()

    store(0, normed_v, normed_out)

    load_head.wait()
    lives = [min(PART, voc - h * PART) for h in range(PARTS)]
    head_part = [head.at[h * PART : h * PART + lives[h]] for h in range(PARTS)]
    own_group = pl.ds(pl.multiple_of(vy * 16, 16), 16)
    lp[PARTS - 1, :, PART - 128 :] = jnp.zeros((ROWS, 128), F32)

    def group(d):
        return pl.ds(pl.multiple_of(ys[d] * 16, 16), 16)

    ways = ((0, 1, 2, 3, slice(0, PART // 2)), (1, 7, 6, 5, slice(PART // 2, PART)))
    c1 = {}

    def first_sends(h):
        lp[h, :, : lives[h]] = lax.dot_general(
            normed, head_part[h][...], (((1,), (1,)), ((), ())), preferred_element_type=F32
        )
        for w, _, two, three, part4 in ways:
            i = 4 * h + 2 * w
            c1[h, w, 0] = start(
                copy(lp.at[h, group(4), part4], relay4.at[h, w], rl_s.at[i], rl_r.at[i], at_y(two))
            )
            c1[h, w, 1] = start(
                copy(lp.at[h, group(three)], relay.at[h, w], rl_s.at[i + 1], rl_r.at[i + 1], at_y(two))
            )

    for h in range(PARTS):
        first_sends(h)
    cl = {}

    def pass_on(h):
        for w, one, two, _, part4 in ways:
            i = 4 * h + 2 * w
            c1[h, w, 0].wait_recv()
            lp[h, group(two), part4] += relay4[h, w]
            cl[h, w, 0] = start(
                copy(lp.at[h, group(two)], lrecv.at[h, 2 * w], lg_s.at[i], lg_r.at[i], at_y(two))
            )
            c1[h, w, 1].wait_recv()
            lp[h, group(one)] += relay[h, w]
            cl[h, w, 1] = start(
                copy(lp.at[h, group(one)], lrecv.at[h, 2 * w + 1], lg_s.at[i + 1], lg_r.at[i + 1], at_y(one))
            )

    is_target = []
    for h in range(PARTS):
        entry = iota((ROWS, PART), 1) + h * PART
        is_target.append((entry + ctx * voc == tgt_c) & (entry < voc))

    def over_vocab(left):
        return sum(
            jnp.dot(left[h][:, : lives[h]], head_part[h][...], preferred_element_type=F32)
            for h in range(PARTS)
        )

    def split(value, buf):
        for i in range(NX):
            for j in range(2):
                g = (i * 2 + j) * 16
                buf[j, i] = value[g : g + 16].astype(BF16)

    split(over_vocab([jnp.where(t, 1.0, 0.0).astype(BF16) for t in is_target]), tbuf)
    ct = start(copy(tbuf.at[1 - k], tcrecv, t_s.at[0], t_r.at[0], other))
    ct.wait_recv()
    txbuf[...] = (tbuf[k].astype(F32) + tcrecv[...].astype(F32)).astype(BF16)
    ct = {
        d: start(copy(txbuf.at[xs[d]], txrecv.at[x], t_s.at[d], t_r.at[d], at_x(d)))
        for d in (2, 1, 3)
    }
    txrecv[x] = txbuf[x]
    for h in range(PARTS):
        pass_on(h)
    to_lane = iota((16, ROWS), 1) == vy * 16 + iota((16, ROWS), 0)
    target16 = rows16(tgt_l, vy * 16).astype(jnp.int32) - ctx * voc
    stat_rows = []
    ce = {}
    for h in range(PARTS):
        for w in range(2):
            cl[h, w, 0].wait_recv()
            cl[h, w, 1].wait_recv()
        logits = lp[h, own_group]
        for i in range(4):
            logits = logits + lrecv[h, i]
        lane = iota((16, PART), 1)
        live = lane < lives[h]
        top = jnp.max(jnp.where(live, logits, -jnp.inf), axis=1, keepdims=True)
        shifted = logits - top
        exps = jnp.where(live, jnp.exp(shifted), 0.0)
        at_target = live & (lane + h * PART == target16)
        e_all[h, own_group] = jnp.where(at_target, 0.0, exps).astype(BF16)
        stat = (
            top,
            jnp.sum(exps, axis=1, keepdims=True),
            jnp.sum(exps * shifted, axis=1, keepdims=True),
            jnp.sum(jnp.where(at_target, logits, 0.0), axis=1, keepdims=True),
        )
        stat_rows += [jnp.sum(jnp.where(to_lane, v, 0.0), axis=0, keepdims=True) for v in stat]
        if h == PARTS - 1:
            st_y[vy] = jnp.concatenate([stack_rows(*stat_rows[i : i + 8]) for i in range(0, 4 * PARTS, 8)], axis=0)
            cy = to_line(FAR_FIRST, vy, at_y, st_y, st_s, st_r, 0)
        for d in FAR_FIRST:
            ce[h, d] = start(
                copy(
                    e_all.at[h, own_group], e_all.at[h, own_group],
                    e_s.at[8 * h + d], e_r.at[8 * h + d], at_y(d),
                )
            )

    for d in range(1, NX):
        ct[d].wait_recv()
    of_targets = jnp.sum(txrecv[...].astype(F32), axis=0)
    for j in range(NZ):
        tzbuf[j] = of_targets[:, j * 128 : (j + 1) * 128].astype(BF16)
    ct = {
        d: start(copy(tzbuf.at[zs[d]], tzrecv.at[z], t_s.at[8 + d], t_r.at[8 + d], at_z(d)))
        for d in FAR_FIRST
    }
    tzrecv[z] = tzbuf[z]

    for d in range(1, NY):
        cy[d].wait_recv()
    block = jnp.sum(st_y[...], axis=0)
    tops = [block[4 * h : 4 * h + 1] for h in range(PARTS)]
    here = combine([block[4 * h : 4 * h + 4] for h in range(PARTS)])
    st_c[k] = here
    cst = start(copy(st_c.at[k], st_c.at[k], st_s.at[20], st_r.at[20], other))

    u = None
    scales = columns(*(jnp.exp(t - here[0:1]) for t in tops))
    for h in range(PARTS):
        for d in range(1, NY):
            ce[h, d].wait_recv()
        left = (scales[h] * e_all[h].astype(F32)).astype(BF16)
        part = jnp.dot(left[:, : lives[h]], head_part[h][...], preferred_element_type=F32)
        u = part if u is None else u + part
    split(u, ubuf)
    cu = start(copy(ubuf.at[1 - k], crecv, u_s.at[0], u_r.at[0], other))
    cst.wait_recv()
    by_core = combine([st_c[0], st_c[1]])
    st_x[x] = by_core
    cx = to_line((2, 1, 3), x, at_x, st_x, st_s, st_r, 16)
    own_l = jnp.exp(here[0:1] - by_core[0:1])
    other_l = jnp.exp(st_c[1 - k][0:1] - by_core[0:1])
    own_s = [rows16(own_l, (2 * i + k) * 16) for i in range(NX)]
    other_s = [rows16(other_l, (2 * i + k) * 16) for i in range(NX)]
    cu.wait_recv()
    for i in range(NX):
        xbuf[i] = (own_s[i] * ubuf[k, i].astype(F32) + other_s[i] * crecv[i].astype(F32)).astype(BF16)
    cu = {
        d: start(copy(xbuf.at[xs[d]], xrecv.at[x], u_s.at[d], u_r.at[d], at_x(d)))
        for d in (2, 1, 3)
    }
    xrecv[x] = xbuf[x]
    for d in range(1, NX):
        cx[d].wait_recv()
    by_x = combine([st_x[i] for i in range(NX)])
    st_z[z] = by_x
    cz = to_line(FAR_FIRST, z, at_z, st_z, st_s, st_r, 8)
    first = (x * 2 + k) * 16
    r0 = pl.ds(pl.multiple_of(first, 16), 16)
    c0 = pl.ds(pl.multiple_of(z * 128, 128), 128)
    scales = [rows16(jnp.exp(st_x[i][0:1] - by_x[0:1]), first) for i in range(NX)]
    inv16 = rows16(inv_l, first)
    for d in range(1, NX):
        cu[d].wait_recv()
    part = scales[0] * xrecv[0].astype(F32)
    for i in range(1, NX):
        part = part + scales[i] * xrecv[i].astype(F32)
    for j in range(NZ):
        zbuf[j] = part[:, j * 128 : (j + 1) * 128].astype(BF16)
    cu = {
        d: start(copy(zbuf.at[zs[d]], zrecv.at[z], u_s.at[8 + d], u_r.at[8 + d], at_z(d)))
        for d in FAR_FIRST
    }
    zrecv[z] = zbuf[z]
    for d in range(1, NZ):
        cz[d].wait_recv()
    whole = combine([st_z[i] for i in range(NZ)])

    lanes1 = iota((1, ROWS), 1)
    den = jnp.where(lanes1 < SEQ_ROWS, den_ref[0], den_ref[1]).astype(F32)
    num = jnp.where(lanes1 < SEQ_ROWS, num_ref[0], num_ref[1]).astype(F32)
    factor = den / (num * (2.0 * MODEL))
    log_total = whole[0:1] + jnp.log(whole[1:2])
    target_l = whole[3:4]
    scaled = LOSS_SCALE * factor
    t_l = scaled * (jnp.exp(target_l - log_total) - 1.0)
    t16 = rows16(t_l, first)
    part = rows16(scaled * jnp.exp(by_x[0:1] - log_total), first) * part + t16 * of_targets
    gain_part = jnp.sum(part * rows[r0, :] * inv16, axis=0, keepdims=True)
    gg_p[x, z] = stack_rows(*(gain_part[:, j * 128 : (j + 1) * 128] for j in range(NZ)))
    cgg = to_plane(gg_p, ggp_s, ggp_r)

    loss = jnp.sum(factor * (log_total - target_l), axis=1, keepdims=True)
    small[8:16] = jnp.broadcast_to(loss, (8, ROWS))
    scales = [rows16(scaled * jnp.exp(st_z[i][0:1] - log_total), first) for i in range(NZ)]
    inner = scaled * (whole[2:3] / whole[1:2] + (whole[0:1] - target_l)) / (inv_l * float(MODEL))
    inner16 = rows16(inv_l * inv_l * inv_l * inner, first)
    for d in range(1, NZ):
        ct[d].wait_recv()
    of_targets = t16 * jnp.sum(tzrecv[...].astype(F32), axis=0)
    turned = inv16 * gain_ref[:, c0]
    taken = rows[r0, c0] * inner16
    for d in range(1, NZ):
        cu[d].wait_recv()
    dn = of_targets
    for i in range(NZ):
        dn = dn + scales[i] * zrecv[i].astype(F32)
    rg = turned * dn - taken
    xl = lax.rem(x, 2)
    rgall[xl, k, z] = rg.astype(BF16)
    mine = rgall.at[xl, k, z]
    cg = {}
    for d in FAR_FIRST:
        cg[d] = start(copy(mine, mine, g_s.at[d], g_r.at[d], at_z(d)))
    for d in FAR_FIRST + (0,):
        cg[8 + d] = start(copy(mine, mine, g_s.at[8 + d], g_r.at[8 + d], at_pair(d)))
    t_c, *w_c = columns(t_l, *(scaled * jnp.exp(t - log_total) for t in tops))
    for h in range(PARTS):
        dl = jnp.where(is_target[h], t_c, w_c[h] * e_all[h].astype(F32))
        dlt[h * PART : (h + 1) * PART] = dl.T.astype(BF16)
    store(1, dlt, dlt_out)
    for c in cgg:
        c.wait_recv()
    ggc[k] = jnp.sum(gg_p[...].reshape(NX * NZ, 8, 128), axis=0)
    cgc = start(copy(ggc.at[k], ggc.at[k], gg_s.at[0], gg_r.at[0], other))
    for c in cg.values():
        c.wait_recv()
    cgr = start(copy(rgall.at[:, k], rgall.at[:, k], g_s.at[16], g_r.at[16], other))
    cgc.wait_recv()
    small[0:8] = ggc[0] + ggc[1]
    store(2, small, small_out)
    for c in sent[:-1]:
        c.wait_send()
    cgr.wait_recv()
    store(3, rgall, rg_out)
    cgr.wait_send()
    for c in stores:
        c.wait()


def final_kernel(
    dlt_hbm, normed_hbm, rg_hbm, small_hbm, pos_hbm, gh_out, gx_out, gg_out, loss_out,
    dlt, normed, rg, small, pos_ref, gh, gx, sems,
):
    loads = []
    for i, (a, b) in enumerate(
        ((dlt_hbm, dlt), (normed_hbm, normed), (pos_hbm, pos_ref), (rg_hbm, rg), (small_hbm, small))
    ):
        loads.append(pltpu.make_async_copy(a, b, sems.at[i]))
        loads[-1].start()
    ctx = lax.axis_index("ctx")
    voc = gh.shape[0]
    for c in loads[:2]:
        c.wait()
    stores = []
    step = WIDTH // 2
    for i in range(2):
        c = slice(i * step, (i + 1) * step)
        gh[:, c] = jnp.dot(dlt[:voc], normed[:, c], preferred_element_type=F32).astype(BF16)
        stores.append(pltpu.make_async_copy(gh.at[:, c], gh_out.at[:, c], sems.at[8 + i]))
        stores[-1].start()
    for c in loads[2:]:
        c.wait()
    pos = jnp.where(ctx < 32, pos_ref[0:1], pos_ref[1:2])
    local = pos - (ctx % 32) * TOK
    spread = jnp.where(iota((TOK, SEQ_ROWS), 0) == local, 1.0, 0.0).astype(BF16)
    for j in range(NZ):
        piece = rg[:, :, j].reshape(SEQ_ROWS, 128)
        gx[:, j * 128 : (j + 1) * 128] = jnp.dot(spread, piece, preferred_element_type=F32).astype(BF16)
    stores.append(pltpu.make_async_copy(gx, gx_out, sems.at[5]))
    stores[-1].start()
    stores.append(pltpu.make_async_copy(small.at[0:8], gg_out, sems.at[6]))
    stores[-1].start()
    loss_out[0, 0] = small[8, 0]
    for c in stores:
        c.wait()


def on_device(hidden, norm_gain, head, masked_pos, masked_targets, t_num, t_den):
    voc = head.shape[0]
    sm = pl.BlockSpec(memory_space=pltpu.SMEM)
    hbm = pl.BlockSpec(memory_space=pltpu.HBM)
    V = pltpu.VMEM
    D = pltpu.SemaphoreType.DMA
    S = pltpu.SMEM
    I32 = jnp.int32
    shape = jax.ShapeDtypeStruct
    dlt, normed, rg, small = pl.pallas_call(
        main_kernel,
        name="main",
        out_shape=(
            shape((PARTS * PART, ROWS), BF16),
            shape((ROWS, WIDTH), BF16),
            shape((2, 2, NZ, 16, 128), BF16),
            shape((16, 128), F32),
        ),
        in_specs=[hbm] * 7,
        out_specs=(hbm,) * 4,
        scratch_shapes=[
            V((TOK, WIDTH), BF16), V((1, WIDTH), F32), V((voc, WIDTH), BF16),
            V((2, SEQ_ROWS), I32), V((2, SEQ_ROWS), I32), S((2,), I32), S((2,), I32),
            V((NX, 2, NZ, 16, WIDTH // 2), BF16),
            V((ROWS, WIDTH), F32),
            V((PARTS, ROWS, PART), F32),
            V((PARTS, 2, 16, PART), F32),
            V((PARTS, 2, 16, PART // 2), F32),
            V((PARTS, 4, 16, PART), F32),
            V((PARTS, ROWS, PART), BF16),
            V((NY, 1, 128), F32), V((NZ, 1, 128), F32), V((NX, 1, 128), F32), V((2, 1, 128), F32),
            V((NY, 4 * PARTS, 128), F32), V((NZ, 8, 128), F32), V((NX, 8, 128), F32), V((2, 8, 128), F32),
            V((2, NX, 16, WIDTH), BF16), V((NX, 16, WIDTH), BF16),
            V((NX, 16, WIDTH), BF16), V((NX, 16, WIDTH), BF16),
            V((NZ, 16, 128), BF16), V((NZ, 16, 128), BF16),
            V((2, NX, 16, WIDTH), BF16), V((NX, 16, WIDTH), BF16),
            V((NX, 16, WIDTH), BF16), V((NX, 16, WIDTH), BF16),
            V((NZ, 16, 128), BF16), V((NZ, 16, 128), BF16),
            V((2, 2, NZ, 16, 128), BF16),
            V((NX, NZ, 8, 128), F32), V((2, 8, 128), F32),
            V((PARTS * PART, ROWS), BF16), V((ROWS, WIDTH), BF16), V((16, 128), F32),
            D((8,)),
            D((8,)), D((8,)), D((8, 4)), D((8, 4)), D((4,)), D((4,)),
            D((24,)), D((24,)), D((24,)), D((24,)),
            D((4 * PARTS,)), D((4 * PARTS,)), D((4 * PARTS,)), D((4 * PARTS,)), D((8 * PARTS,)), D((8 * PARTS,)),
            D((20,)), D((20,)), D((16,)), D((16,)), D((17,)), D((17,)), D((1,)), D((1,)), D((NX, NZ)), D((NX, NZ)),
        ],
        compiler_params=pltpu.CompilerParams(
            collective_id=0, has_side_effects=True, vmem_limit_bytes=60 << 20
        ),
    )(hidden, norm_gain.reshape(1, WIDTH), head, masked_pos, masked_targets, t_num, t_den)
    grad_head, grad_hidden, grad_gain, loss_value = pl.pallas_call(
        final_kernel,
        name="final",
        out_shape=(
            shape((voc, WIDTH), BF16),
            shape((TOK, WIDTH), BF16),
            shape((8, 128), F32),
            shape((1, 1), F32),
        ),
        in_specs=[hbm] * 5,
        out_specs=(hbm, hbm, hbm, sm),
        scratch_shapes=[
            V((PARTS * PART, ROWS), BF16), V((ROWS, WIDTH), BF16), V((2, 2, NZ, 16, 128), BF16),
            V((16, 128), F32), V((2, SEQ_ROWS), I32),
            V((voc, WIDTH), BF16), V((TOK, WIDTH), BF16), D((12,)),
        ],
        compiler_params=pltpu.CompilerParams(vmem_limit_bytes=60 << 20),
    )(dlt, normed, rg, small, masked_pos)
    return (loss_value.reshape(()), grad_hidden, grad_head, grad_gain.reshape(WIDTH))


def solution(mesh):
    placed = (P("ctx", "vocab"), P("vocab"), P("ctx", "vocab"), P(), P(), P(), P())
    return jax.shard_map(
        on_device,
        mesh=mesh,
        in_specs=placed,
        out_specs=(P(), P("ctx", "vocab"), P("ctx", "vocab"), P("vocab")),
        check_vma=False,
    )
```
